32 devices in a mesh: slide: 4 (over z), ctx: 8 (over y, x, core).
Axes of the slice: x: 2, y: 2, z: 4, core: 2. Of those that a mesh axis runs over, the one named last changes fastest.
Arguments:
- tiles: bfloat16 [4, 4096, 768], P('slide', 'ctx'), may hold values from -40 to 40
- tile_pos: int32 [4, 4096], P('slide', 'ctx'), may hold values from 0 to 4095, as said below
- lengths: int32 [4], P('slide'), may hold values from 1024 to 4096, as said below
- qkv_weight: bfloat16 [768, 1152], replicated, may hold values from -0.21875 to 0.21875
- out_weight: bfloat16 [384, 768], replicated, may hold values from -0.3125 to 0.3125
- cotangent: bfloat16 [4, 4096, 768], P('slide', 'ctx'), may hold values from -6 to 6
Outputs:
- tile_grads: bfloat16 [4, 4096, 768], P('slide', 'ctx')
- out_weight_grad: float32 [294912], P(('slide', 'ctx'))
- far_kv_grads: float32 [4, 2, 6, 256, 64], P('slide', None, None, 'ctx')
The draws below stay inside these ranges and needn't reach their ends.
Inputs may be any that keep to these rules, and one draw needn't show every extreme that they name: `tile_pos`: for every slide the entries are a permutation of its 4096 positions; the 512 entries held by one device of ctx contain exactly 64 positions of each block of 512 consecutive positions, in no particular order. `lengths`: at least one slide has all 4096 positions live.
All inputs are finite; a program needn't handle non-finite values.
Results may differ from the reference program's by a relative error of at most 0.014.
The reference program's roundings to bfloat16 on the way count: a program that leaves them out, or rounds other values in their place, can miss the bound.
Values may be sent and summed in bfloat16 or wider, within the bound.
A program may use at most 128 MiB of HBM per device.

```python
import math
import jax
import jax.numpy as jnp
from jax import lax

D = 768
HEAD_COUNT = 6
HD = 64
WIDE_RATE2 = 16
TOK_DEV = 512
SLOT_COUNT = 4096
SLIDES = 4
PORTION = 64
N_CTX = 8


def draw_tiles(key, part):
    key = jax.random.fold_in(key, 5)
    first = jax.random.fold_in(key, 0)
    values = jax.random.normal(first, (SLIDES, SLOT_COUNT, D), jnp.float32)
    return jnp.clip(values, -40.0, 40.0).astype(jnp.bfloat16)


def shuffle_one(subkey):
    return jax.random.permutation(subkey, TOK_DEV).astype(jnp.int32)


def draw_tile_pos(key, part):
    key = jax.random.fold_in(key, 11)
    first, second = jax.random.split(key, 2)
    within = jax.vmap(shuffle_one)(jax.random.split(first, SLIDES * N_CTX)).reshape(SLIDES, N_CTX, TOK_DEV)
    within = within + (jnp.arange(N_CTX, dtype=jnp.int32) * TOK_DEV)[None, :, None]
    grouped = within.reshape(SLIDES, N_CTX, N_CTX, PORTION).transpose(0, 2, 1, 3).reshape(SLIDES, N_CTX, TOK_DEV)
    holder = jax.vmap(shuffle_one)(jax.random.split(second, SLIDES * N_CTX)).reshape(SLIDES, N_CTX, TOK_DEV)
    placed = jnp.take_along_axis(grouped, holder, -1)
    return placed.reshape(SLIDES, SLOT_COUNT).astype(jnp.int32)


def draw_lengths(key, part):
    key = jax.random.fold_in(key, 7)
    first, second = jax.random.split(key, 2)
    drawn = jax.random.randint(first, (SLIDES,), SLOT_COUNT // 4, SLOT_COUNT + 1, jnp.int32)
    picked = jax.random.randint(second, (), 0, SLIDES, jnp.int32)
    return jnp.where(jnp.arange(SLIDES) == picked, SLOT_COUNT, drawn).astype(jnp.int32)


def shard_levels(key, dims, cuts, smallest, largest):
    gain = 1.0
    for position, shards_of in cuts:
        steps = jax.random.uniform(jax.random.fold_in(jax.random.fold_in(key, 6), position), (shards_of,), jnp.float32, smallest / len(cuts), largest / len(cuts))
        gain = gain * jnp.repeat(jnp.exp(steps), dims[position] // shards_of).reshape((-1,) + (1,) * (len(dims) - 1 - position))
    return gain


def scatter_about(stream_key, extent, width, reach, pieces=(), kind=jnp.bfloat16):
    values = jax.random.normal(stream_key, extent, jnp.float32) * width
    if len(pieces) > 0:
        values = shard_levels(stream_key, extent, pieces, -0.22, 0.18) * values
    return jnp.clip(values, min=-reach, max=reach).astype(kind)


def setup_inputs(seed: int = 0) -> dict:
    streams_of = jax.random.split(jax.random.key(seed), 7)
    tiles = draw_tiles(jax.random.fold_in(streams_of[6], 71), 0)
    tile_pos = draw_tile_pos(jax.random.fold_in(streams_of[6], 71), 0)
    lengths = draw_lengths(jax.random.fold_in(streams_of[6], 71), 0)
    qkv_weight = scatter_about(streams_of[3], (D, 3 * HEAD_COUNT * HD), D ** -0.5, 0.21875)
    out_weight = scatter_about(streams_of[4], (HEAD_COUNT * HD, D), (HEAD_COUNT * HD) ** -0.5, 0.3125)
    cotangent = scatter_about(streams_of[5], (SLIDES, SLOT_COUNT, D), 1.0, 6.0, ((0, 4), (1, 8)))
    return dict(tiles=tiles, tile_pos=tile_pos, lengths=lengths, qkv_weight=qkv_weight, out_weight=out_weight, cotangent=cotangent)


NEGATIVE_FLOOR = -1e+30

def dilate(tensor, stride):
    number = tensor.shape[1]
    lattice = tensor.reshape(tensor.shape[0] // stride, stride, number, tensor.shape[2])
    return jnp.stack([lattice[:, offset, offset, :] for offset in range(number)], 0)

def selector(number, stride):
    return jnp.arange(stride)[None, :] == jnp.arange(number)[:, None]

def spread(values, stride, filler):
    chosen = selector(values.shape[0], stride)
    return jnp.where(chosen[:, None, :], values[:, :, None], filler).reshape(values.shape[0], -1)

def spread_rows(values, stride):
    chosen = selector(values.shape[0], stride)
    placed = jnp.where(chosen[:, None, :, None], values[:, :, None, :], 0.0)
    return placed.reshape(values.shape[0], -1, values.shape[2])

def extract(field, stride):
    chosen = selector(field.shape[0], stride)
    lattice = field.reshape(field.shape[0], -1, stride)
    return lax.optimization_barrier(jnp.sum(jnp.where(chosen[:, None, :], lattice, 0.0), -1))

def extract_rows(field, stride):
    chosen = selector(field.shape[0], stride)
    lattice = field.reshape(field.shape[0], -1, stride, field.shape[2])
    return lax.optimization_barrier(jnp.sum(jnp.where(chosen[:, None, :, None], lattice, 0.0), 2))

def rounded(values):
    return lax.optimization_barrier(values.astype(jnp.bfloat16)).astype(jnp.float32)

def by_heads(values, segments):
    return values.transpose(1, 0, 2, 3).reshape(HEAD_COUNT, SLOT_COUNT, HD)

def slide_pass(sequence, grad_seq, slide_length, qkv_weight, out_weight):
    segments = SLOT_COUNT // TOK_DEV
    projected = jnp.dot(sequence, qkv_weight, preferred_element_type=jnp.float32)
    projected = rounded(projected).reshape(SLOT_COUNT, 3, HEAD_COUNT, HD)
    queries = projected[:, 0]
    keyset = projected[:, 1]
    values = projected[:, 2]
    live_rows = jnp.arange(SLOT_COUNT) < slide_length
    seg_query = queries.reshape(segments, TOK_DEV, HEAD_COUNT, HD)
    seg_keys = keyset.reshape(segments, TOK_DEV, HEAD_COUNT, HD)
    seg_values = values.reshape(segments, TOK_DEV, HEAD_COUNT, HD)
    seg_live = live_rows.reshape(segments, 1, 1, TOK_DEV)
    local_scores = jnp.einsum('nqhd,nkhd->nhqk', seg_query, seg_keys) * 0.125
    local_masked = jnp.where(seg_live, local_scores, NEGATIVE_FLOOR)
    local_max = lax.optimization_barrier(jnp.max(local_masked, -1)).transpose(1, 0, 2).reshape(HEAD_COUNT, SLOT_COUNT)
    near_query = dilate(queries, WIDE_RATE2)
    near_keys = dilate(keyset, WIDE_RATE2)
    near_values = dilate(values, WIDE_RATE2)
    dilated_positions = jnp.arange(SLOT_COUNT // WIDE_RATE2)[None, :] * WIDE_RATE2 + jnp.arange(HEAD_COUNT)[:, None]
    dilated_live_mask = dilated_positions < slide_length
    distant_scores = jnp.einsum('hqd,hkd->hqk', near_query, near_keys) * 0.125
    distant_masked = jnp.where(dilated_live_mask[:, None, :], distant_scores, NEGATIVE_FLOOR)
    far_max = lax.optimization_barrier(jnp.max(distant_masked, -1))
    ceiling = jnp.maximum(local_max, spread(far_max, WIDE_RATE2, NEGATIVE_FLOOR))
    seg_ceiling = ceiling.reshape(HEAD_COUNT, segments, TOK_DEV).transpose(1, 0, 2)
    local_weights = jnp.where(seg_live, jnp.exp(local_masked - seg_ceiling[..., None]), 0.0)
    distant_ceiling = extract(ceiling, WIDE_RATE2)
    distant_weights = jnp.where(dilated_live_mask[:, None, :], jnp.exp(distant_masked - distant_ceiling[:, :, None]), 0.0)
    local_sums = lax.optimization_barrier(jnp.sum(local_weights, -1)).transpose(1, 0, 2).reshape(HEAD_COUNT, SLOT_COUNT)
    totals = local_sums + spread(lax.optimization_barrier(jnp.sum(distant_weights, -1)), WIDE_RATE2, 0.0)
    local_numer = by_heads(jnp.einsum('nhqk,nkhd->nhqd', rounded(local_weights), seg_values), segments)
    numerator = local_numer + spread_rows(jnp.einsum('hqk,hkd->hqd', rounded(distant_weights), near_values), WIDE_RATE2)
    divisor = jnp.where(live_rows[None, :], totals, 1.0)
    result = jnp.where(live_rows[None, :, None], numerator / divisor[:, :, None], 0.0)
    attention = result.transpose(1, 0, 2).reshape(SLOT_COUNT, HEAD_COUNT * HD).astype(jnp.bfloat16)
    partial_term = jnp.dot(attention.T, grad_seq, preferred_element_type=jnp.float32)
    grad_attn = jnp.dot(grad_seq, out_weight.T, preferred_element_type=jnp.float32)
    grad_attn = rounded(grad_attn).reshape(SLOT_COUNT, HEAD_COUNT, HD)
    grad_out = jnp.where(live_rows[:, None, None], grad_attn, 0.0).transpose(1, 0, 2)
    inner_stat = lax.optimization_barrier(jnp.sum(grad_out * result, -1))
    seg_divisor = divisor.reshape(HEAD_COUNT, segments, TOK_DEV).transpose(1, 0, 2)
    seg_stat = inner_stat.reshape(HEAD_COUNT, segments, TOK_DEV).transpose(1, 0, 2)
    seg_grad = grad_out.reshape(HEAD_COUNT, segments, TOK_DEV, HD).transpose(1, 0, 2, 3)
    local_prob = local_weights / seg_divisor[..., None]
    local_dprob = jnp.einsum('nhqd,nkhd->nhqk', seg_grad, seg_values)
    local_dscore = rounded(local_prob * (local_dprob - seg_stat[..., None]) * 0.125)
    grad_query = by_heads(jnp.einsum('nhqk,nkhd->nhqd', local_dscore, seg_keys), segments)
    grad_key = by_heads(jnp.einsum('nhqk,nqhd->nhkd', local_dscore, seg_query), segments)
    grad_value = by_heads(jnp.einsum('nhqk,nhqd->nhkd', rounded(local_prob), seg_grad), segments)
    near_divisor = extract(divisor, WIDE_RATE2)
    near_stat = extract(inner_stat, WIDE_RATE2)
    near_grad = extract_rows(grad_out, WIDE_RATE2)
    far_prob = distant_weights / near_divisor[:, :, None]
    far_dprob = jnp.einsum('hqd,hkd->hqk', near_grad, near_values)
    far_dscore = rounded(far_prob * (far_dprob - near_stat[:, :, None]) * 0.125)
    far_kgrad = jnp.einsum('hqk,hqd->hkd', far_dscore, near_query)
    far_vgrad = jnp.einsum('hqk,hqd->hkd', rounded(far_prob), near_grad)
    grad_query = grad_query + spread_rows(jnp.einsum('hqk,hkd->hqd', far_dscore, near_keys), WIDE_RATE2)
    grad_key = grad_key + spread_rows(far_kgrad, WIDE_RATE2)
    grad_value = grad_value + spread_rows(far_vgrad, WIDE_RATE2)
    far_pair = jnp.stack([far_kgrad, far_vgrad], 0) * math.sqrt(SLOT_COUNT // WIDE_RATE2)
    stacked = jnp.stack([grad_query, grad_key, grad_value], 0).transpose(2, 0, 1, 3)
    stacked = stacked.reshape(SLOT_COUNT, 3 * HEAD_COUNT * HD).astype(jnp.bfloat16)
    grad_tiles = jnp.dot(stacked, qkv_weight.T, preferred_element_type=jnp.float32).astype(jnp.bfloat16)
    return (grad_tiles, partial_term, far_pair)

def reference(tiles, tile_pos, lengths, qkv_weight, out_weight, cotangent):

    def one_slide(bundle):
        owned, places, slide_length, grad_seq = bundle
        sequence = jnp.zeros_like(owned).at[places].set(owned)
        grad_tiles, partial_term, far_pair = slide_pass(sequence, grad_seq, slide_length, qkv_weight, out_weight)
        return (grad_tiles[places], partial_term, far_pair)
    backs, terms, far_pairs = lax.map(one_slide, (tiles, tile_pos, lengths, cotangent))
    factor = 1.0 / math.sqrt(SLIDES * SLOT_COUNT)
    weight_grad = lax.optimization_barrier(jnp.sum(terms * factor, 0)).reshape(-1)
    return (backs, weight_grad, far_pairs.astype(jnp.float32))
```

```python
import functools
import math

import jax
import jax.numpy as jnp
from jax import lax
from jax.experimental import pallas as pl
from jax.experimental.pallas import tpu as pltpu
from jax.sharding import PartitionSpec as P

HD = 64
STRIDE = 16
FLOOR = -1e30
BF = jnp.bfloat16
F32 = jnp.float32
HIGH = lax.Precision.HIGHEST
MESH = pl.DeviceIdType.MESH


def dot(a, b):
    return lax.dot_general(a, b, (((1,), (0,)), ((), ())), preferred_element_type=F32)


def dot_t(a, b):
    return lax.dot_general(a, b, (((1,), (1,)), ((), ())), preferred_element_type=F32)


def exact_dot(a, b, last):
    return lax.dot_general(
        a, b, (((1,), (last,)), ((), ())), precision=HIGH, preferred_element_type=F32
    )


def flip(x):
    return x.astype(F32).T.astype(BF)


def halves(x):
    high = x.astype(BF)
    return high, (x - high.astype(F32)).astype(BF)


def iota(shape, dim):
    return lax.broadcasted_iota(jnp.int32, shape, dim)


def hot(cond):
    return jnp.where(cond, 1.0, 0.0).astype(BF)


def column(row):
    return jnp.broadcast_to(row, (128, row.shape[1])).T[:, :1]


def layer(n, slides, fused, len_ref, pos_ref, tiles_ref, wqkv_ref, wout_ref, cot_ref,
          grads_ref, wgrad_ref, far_ref,
          sent, psend, got, pbuf, slot_ref, st_ref, rt_ref, proj, g_ref, gt_ref, kt_ref, vt_ref,
          w_ref, dp_ref, m_ref, l_ref, nt_ref, att_ref, stat_ref, fbuf, gbuf, stats, sbuf,
          dqt_ref, dk_ref, dv_ref, bsend, bbuf, pw, wbuf, zs, zbuf,
          send_sems, recv_sems, zsend, zrecv):
    me = lax.axis_index("ctx")
    my_slide = lax.axis_index("slide")
    t, d = tiles_ref.shape
    hc = wout_ref.shape[0]
    heads = hc // HD
    portion = t // n
    g = t // STRIDE
    fq = heads * g
    nf = n * g

    barrier = pltpu.get_barrier_semaphore()

    def greet(k, carry):
        pl.semaphore_signal(barrier, inc=1, device_id={"ctx": lax.rem(me + k, n)},
                            device_id_type=MESH)
        return carry

    lax.fori_loop(1, n, greet, 0)
    if fused:
        for k in range(1, slides):
            pl.semaphore_signal(barrier, inc=1,
                                device_id={"slide": lax.rem(my_slide + k, slides)},
                                device_id_type=MESH)

    def copy_to(which, k, src, dst):
        return pltpu.make_async_remote_copy(
            src_ref=src, dst_ref=dst, send_sem=send_sems.at[which, k],
            recv_sem=recv_sems.at[which, k], device_id={"ctx": lax.rem(me + k, n)},
            device_id_type=MESH)

    def push(which, source, target):
        def body(k, carry):
            copy_to(which, k, source(lax.rem(me + k, n)), target.at[me]).start()
            return carry
        lax.fori_loop(1, n, body, 0)

    def landed(which, target):
        def body(k, carry):
            owner = lax.rem(me + n - k, n)
            copy_to(which, k, target.at[owner], target.at[owner]).wait_recv()
            return carry
        lax.fori_loop(1, n, body, 0)

    def left(which, target):
        def body(k, carry):
            copy_to(which, k, target.at[0], target.at[0]).wait_send()
            return carry
        lax.fori_loop(1, n, body, 0)

    length = len_ref[0]

    prow = pos_ref[...].astype(F32)
    pcol = column(prow)
    rank = jnp.sum(jnp.where(pcol < prow, 1.0, 0.0), axis=0, keepdims=True)
    down = iota((t, t), 0).astype(F32)
    across = iota((t, t), 1).astype(F32)
    sent[...] = dot(hot(rank == down), tiles_ref[...]).astype(BF).reshape(n, portion, d)
    placed = column(rank) == across
    st_ref[...] = hot(placed)
    ordered = jnp.sum(jnp.where(placed, pcol, 0.0), axis=0, keepdims=True)
    psend[...] = jnp.zeros_like(psend)
    for k in range(n):
        psend[k, :, 0:portion] = jnp.broadcast_to(
            ordered[:, k * portion:(k + 1) * portion], (8, portion))
    pl.semaphore_wait(barrier, n - 1 + (slides - 1 if fused else 0))
    push(1, lambda peer: psend.at[peer], pbuf)
    push(0, lambda peer: sent.at[peer], got)
    got[me] = sent[me]
    pbuf[me] = psend[me]

    base = me * t
    live_row = base + iota((1, t), 1) < length
    live_col = base + iota((t, 1), 0) < length
    grad_rows = jnp.where(live_col, dot_t(cot_ref[...], wout_ref[...]), 0.0)
    g_ref[...] = grad_rows.astype(BF)
    gt_ref[...] = jnp.where(live_row, dot_t(wout_ref[...], cot_ref[...]), 0.0).astype(BF)
    gather = hot(iota((g, t), 1) // STRIDE == iota((g, t), 0))
    own_head = iota((t, hc), 0) % STRIDE == iota((t, hc), 1) // HD
    gbuf[me] = dot(gather, jnp.where(own_head, grad_rows, 0.0).astype(BF)).astype(BF)
    push(2, lambda peer: gbuf.at[me], gbuf)

    landed(1, pbuf)
    for k in range(n):
        slot_ref[:, k * portion:(k + 1) * portion] = pbuf[k, :, 0:portion]
    slot = slot_ref[0:1, :] - (me * t).astype(F32)
    rt_ref[...] = hot(column(slot) == across)
    put = hot(slot == down)
    landed(0, got)
    sequence = dot(put, got[...].reshape(t, d)).astype(BF)
    for k in range(3):
        cols = slice(k * hc, (k + 1) * hc)
        part = dot(sequence, wqkv_ref[:, cols])
        rounded = part.astype(BF)
        proj[:, cols] = rounded
        fbuf[me, :, cols] = dot(gather, jnp.where(own_head, part, 0.0).astype(BF)).astype(BF)
        if k == 1:
            kt_ref[...] = flip(rounded)
        if k == 2:
            vt_ref[...] = flip(rounded)
    push(3, lambda peer: fbuf.at[me], fbuf)

    m_ref[...] = jnp.zeros_like(m_ref)
    l_ref[...] = jnp.zeros_like(l_ref)
    stat_ref[...] = jnp.zeros_like(stat_ref)
    lane = iota((1, 2 * HD), 1)

    for pair in range(heads // 2):
        cols = slice(pair * 128, pair * 128 + 128)
        q2 = proj[:, cols]
        k2 = proj[:, hc + pair * 128:hc + pair * 128 + 128]
        v2 = proj[:, 2 * hc + pair * 128:2 * hc + pair * 128 + 128]
        for half in range(2):
            h = 2 * pair + half
            rows = slice(h * HD, h * HD + HD)
            mine = hot(lane // HD == half)
            score = jnp.where(live_col, dot_t(k2 * mine, q2) * 0.125, FLOOR)
            top = jnp.max(score, axis=0, keepdims=True)
            weight = jnp.where(live_col, jnp.exp(score - top), 0.0)
            w_ref[h] = weight
            m_ref[h:h + 1, :] = top
            l_ref[h:h + 1, :] = jnp.sum(weight, axis=0, keepdims=True)
            nt_ref[rows, :] = dot(vt_ref[rows, :], weight.astype(BF))
            dp_ref[h] = dot(v2 * mine, gt_ref[cols, :])

    landed(2, gbuf)
    landed(3, fbuf)
    all_q = fbuf[:, :, 0:hc].reshape(nf, hc)
    all_k = fbuf[:, :, hc:2 * hc].reshape(nf, hc)
    all_v = fbuf[:, :, 2 * hc:3 * hc].reshape(nf, hc)
    all_g = gbuf[...].reshape(nf, hc)
    block = hot(iota((fq, hc), 0) // g == iota((fq, hc), 1) // HD)

    def diagonal(x):
        return jnp.concatenate([x] * heads, axis=0) * block

    own_q = diagonal(fbuf[me, :, 0:hc])
    own_k = diagonal(fbuf[me, :, hc:2 * hc])
    own_v = diagonal(fbuf[me, :, 2 * hc:3 * hc])
    own_g = diagonal(gbuf[me])
    place = iota((fq, t), 1) == (iota((fq, t), 0) % g) * STRIDE + iota((fq, t), 0) // g
    spread = jnp.where(place, 1.0, 0.0)
    spread_bf = spread.astype(BF)
    head_rows = iota((8, fq), 0) == iota((8, fq), 1) // g

    def widen(row):
        return exact_dot(jnp.where(head_rows, row, 0.0), spread, 0)

    def narrow(rows):
        return jnp.sum(jnp.where(head_rows, exact_dot(rows, spread, 1), 0.0), axis=0,
                       keepdims=True)

    def spread_cols(x):
        kept = jnp.where(iota((hc, fq), 0) // HD == iota((hc, fq), 1) // g, x, 0.0)
        high, low = halves(kept)
        return dot(high, spread_bf) + dot(low, spread_bf)

    far_live = iota((nf, fq), 0) * STRIDE + iota((nf, fq), 1) // g < length
    far_score = jnp.where(far_live, dot_t(all_k, own_q) * 0.125, FLOOR)
    far_top = jnp.max(far_score, axis=0, keepdims=True)
    chosen = iota((8, t), 1) % STRIDE == iota((8, t), 0)
    tops = m_ref[...]
    ceiling = jnp.maximum(tops, jnp.where(chosen, widen(far_top), FLOOR))
    rescale = jnp.exp(tops - ceiling)
    far_weight = jnp.where(far_live, jnp.exp(far_score - narrow(ceiling)), 0.0)
    totals = l_ref[...] * rescale + widen(jnp.sum(far_weight, axis=0, keepdims=True))
    inverse = 1.0 / jnp.where(live_row, totals, 1.0)
    inverse = jnp.where(iota((8, t), 0) < heads, inverse, 0.0)
    far_numer = spread_cols(dot(flip(all_v), far_weight.astype(BF)))
    for h in range(heads):
        rows = slice(h * HD, h * HD + HD)
        result = (nt_ref[rows, :] * rescale[h:h + 1] + far_numer[rows, :]) * inverse[h:h + 1]
        result = jnp.where(live_row, result, 0.0)
        att_ref[rows, :] = result.astype(BF)
        stat_ref[h:h + 1, :] = jnp.sum(gt_ref[rows, :].astype(F32) * result, axis=0, keepdims=True)
    stat = stat_ref[...]

    stats[...] = jnp.zeros_like(stats)
    stats[0:8, :] = ceiling
    stats[8:16, :] = inverse
    stats[16:24, :] = stat
    turned = stats[...].T
    wanted = iota((t, 128), 0) % STRIDE == iota((t, 128), 1) % 8
    sbuf[me] = jnp.sum(jnp.where(wanted, turned, 0.0).reshape(g, STRIDE, 128), axis=1)
    push(4, lambda peer: sbuf.at[me], sbuf)

    factor = 1.0 / math.sqrt(slides * n * t)
    if fused:
        run = hc // (n * slides)
        spot = iota((hc, hc), 0)
        source = (spot % (run * slides)) // run * (n * run) + spot // (run * slides) * run + spot % run
        order = hot(iota((hc, hc), 1) == source)
        att = dot(order, att_ref[...]).astype(BF)
        pw[...] = (dot(att, cot_ref[...]) * factor).astype(BF).reshape(n, hc // n, d)
        wbuf[me] = pw[me]
        push(5, lambda peer: pw.at[peer], wbuf)
    else:
        wgrad_ref[...] = dot(att_ref[...], cot_ref[...]) * factor

    for pair in range(heads // 2):
        cols = slice(pair * 128, pair * 128 + 128)
        q2 = proj[:, cols]
        g2 = g_ref[:, cols]
        key_parts = []
        value_parts = []
        for half in range(2):
            h = 2 * pair + half
            rows = slice(h * HD, h * HD + HD)
            prob = w_ref[h] * (rescale[h:h + 1] * inverse[h:h + 1])
            dscore = (prob * (dp_ref[h] - stat[h:h + 1]) * 0.125).astype(BF)
            dqt_ref[rows, :] = dot(kt_ref[rows, :], dscore)
            key_parts.append(dot(dscore, q2))
            value_parts.append(dot(prob.astype(BF), g2))
        dk_ref[:, cols] = jnp.where(lane < HD, key_parts[0], key_parts[1])
        dv_ref[:, cols] = jnp.where(lane < HD, value_parts[0], value_parts[1])

    far_prob = far_weight * narrow(inverse)
    far_dscore = far_prob * (dot_t(all_v, own_g) - narrow(stat)) * 0.125
    dqt = dqt_ref[...] + spread_cols(dot(flip(all_k), far_dscore.astype(BF)))
    proj[:, 0:hc] = dqt.T.astype(BF)
    landed(4, sbuf)
    rows_all = sbuf[...].reshape(nf, 128).T

    def per_head(first):
        return jnp.concatenate(
            [jnp.broadcast_to(rows_all[first + h:first + h + 1], (g, nf)) for h in range(heads)], axis=0)

    key_spot = iota((fq, 1), 0)
    key_live = (me * g + key_spot % g) * STRIDE + key_spot // g < length
    own_score = dot_t(own_k, all_q) * 0.125
    own_weight = jnp.where(key_live, jnp.exp(jnp.where(key_live, own_score - per_head(0), 0.0)), 0.0)
    own_prob = own_weight * per_head(8)
    own_dscore = own_prob * (dot_t(own_v, all_g) - per_head(16)) * 0.125
    scale = math.sqrt(nf)
    back_spread = hot(iota((t, fq), 0)
                      == (iota((t, fq), 1) % g) * STRIDE + iota((t, fq), 1) // g)
    keep = iota((fq, hc), 0) // g == iota((fq, hc), 1) // HD
    for which, left_side, right_side, base_ref in (
        (0, own_dscore, all_q, dk_ref), (1, own_prob, all_g, dv_ref)
    ):
        term = dot(left_side.astype(BF), right_side)
        for h in range(heads):
            far_ref[which, h] = term[h * g:(h + 1) * g, h * HD:(h + 1) * HD] * scale
        high, low = halves(jnp.where(keep, term, 0.0))
        total = base_ref[...] + dot(back_spread, high) + dot(back_spread, low)
        proj[:, (which + 1) * hc:(which + 2) * hc] = total.astype(BF)

    grad_seq = dot_t(proj[...], wqkv_ref[...]).astype(BF)
    bsend[...] = dot(rt_ref[...], grad_seq).astype(BF).reshape(n, portion, d)
    push(6, lambda peer: bsend.at[peer], bbuf)
    bbuf[me] = bsend[me]

    if fused:
        def slide_copy(k, src, dst):
            return pltpu.make_async_remote_copy(
                src_ref=src, dst_ref=dst, send_sem=zsend.at[k], recv_sem=zrecv.at[k],
                device_id={"slide": lax.rem(my_slide + k, slides)}, device_id_type=MESH)

        landed(5, wbuf)
        summed = jnp.sum(wbuf[...].astype(F32), axis=0)
        zs[...] = jnp.zeros_like(zs)
        for k in range(slides):
            zs[k, 0:run, :] = summed[k * run:(k + 1) * run, :]
        for k in range(1, slides):
            slide_copy(k, zs.at[lax.rem(my_slide + k, slides)], zbuf.at[my_slide]).start()
        zbuf[my_slide] = zs[my_slide]

    landed(6, bbuf)
    grads_ref[...] = dot(st_ref[...], bbuf[...].reshape(t, d)).astype(BF)

    if fused:
        for k in range(1, slides):
            owner = lax.rem(my_slide + slides - k, slides)
            slide_copy(k, zbuf.at[owner], zbuf.at[owner]).wait_recv()
        wgrad_ref[...] = jnp.sum(zbuf[...], axis=0)[0:run, :]
        for k in range(1, slides):
            slide_copy(k, zs.at[0], zbuf.at[0]).wait_send()
        left(5, wbuf)
    for which, target in ((0, got), (1, pbuf), (2, gbuf), (3, fbuf), (4, sbuf), (6, bbuf)):
        left(which, target)


def local(slides, n, tiles, tile_pos, lengths, qkv_weight, out_weight, cotangent):
    _, t, d = tiles.shape
    hc = out_weight.shape[0]
    heads = hc // HD
    portion = t // n
    g = t // STRIDE
    fused = hc % (n * slides) == 0 and (hc // n) % 16 == 0
    run = hc // (n * slides) if fused else 0
    pad = -(-run // 8) * 8 if fused else 8
    wrows = hc // n if fused else 16
    vm = pltpu.VMEM
    scratch = [
        vm((n, portion, d), BF), vm((n, 8, 128), F32), vm((n, portion, d), BF),
        vm((n, 8, 128), F32), vm((8, t), F32), vm((t, t), BF), vm((t, t), BF),
        vm((t, 3 * hc), BF), vm((t, hc), BF), vm((hc, t), BF), vm((hc, t), BF), vm((hc, t), BF),
        vm((heads, t, t), F32), vm((heads, t, t), F32), vm((8, t), F32), vm((8, t), F32),
        vm((hc, t), F32), vm((hc, t), BF), vm((8, t), F32),
        vm((n, g, 3 * hc), BF), vm((n, g, hc), BF), vm((128, t), F32), vm((n, g, 128), F32),
        vm((hc, t), F32), vm((t, hc), F32), vm((t, hc), F32),
        vm((n, portion, d), BF), vm((n, portion, d), BF),
        vm((n, wrows, d), BF), vm((n, wrows, d), BF),
        vm((slides, pad, d), F32), vm((slides, pad, d), F32),
        pltpu.SemaphoreType.DMA((7, n)), pltpu.SemaphoreType.DMA((7, n)),
        pltpu.SemaphoreType.DMA((slides,)), pltpu.SemaphoreType.DMA((slides,)),
    ]
    spec = pl.BlockSpec(memory_space=pltpu.VMEM)
    grads, wgrad, far = pl.pallas_call(
        functools.partial(layer, n, slides, fused),
        out_shape=(
            jax.ShapeDtypeStruct((t, d), BF),
            jax.ShapeDtypeStruct((run if fused else hc, d), F32),
            jax.ShapeDtypeStruct((2, heads, g, HD), F32),
        ),
        in_specs=[pl.BlockSpec(memory_space=pltpu.SMEM)] + [spec] * 5,
        out_specs=(spec, spec, spec),
        scratch_shapes=scratch,
        compiler_params=pltpu.CompilerParams(
            collective_id=0, has_side_effects=True, vmem_limit_bytes=56 * 1024 * 1024
        ),
        cost_estimate=pl.CostEstimate(flops=8 * 10**9, bytes_accessed=6 * 10**6, transcendentals=2 * 10**6),
    )(lengths, tile_pos, tiles[0], qkv_weight, out_weight, cotangent[0])
    if fused:
        wgrad = wgrad.reshape(-1)
    else:
        wgrad = lax.psum_scatter(
            wgrad.reshape(-1), ("slide", "ctx"), scatter_dimension=0, tiled=True
        )
    return grads[None], wgrad, far[None]


def solution(mesh):
    placed = (
        P("slide", "ctx", None),
        P("slide", "ctx"),
        P("slide"),
        P(),
        P(),
        P("slide", "ctx", None),
    )
    return jax.shard_map(
        functools.partial(local, mesh.shape["slide"], mesh.shape["ctx"]),
        mesh=mesh,
        in_specs=placed,
        out_specs=(
            P("slide", "ctx", None),
            P(("slide", "ctx")),
            P("slide", None, None, "ctx", None),
        ),
        check_vma=False,
    )
```

```python
import functools
import math

import jax
import jax.numpy as jnp
from jax import lax
from jax.experimental import pallas as pl
from jax.experimental.pallas import tpu as pltpu
from jax.sharding import PartitionSpec as P

HD = 64
STRIDE = 16
FLOOR = -1e30
BF = jnp.bfloat16
F32 = jnp.float32
MESH = pl.DeviceIdType.MESH


def dot(a, b):
    return lax.dot_general(a, b, (((1,), (0,)), ((), ())), preferred_element_type=F32)


def dot_t(a, b):
    return lax.dot_general(a, b, (((1,), (1,)), ((), ())), preferred_element_type=F32)


def flip(x):
    return x.astype(F32).T.astype(BF)


def halves(x):
    high = x.astype(BF)
    return high, (x - high.astype(F32)).astype(BF)


def iota(shape, dim):
    return lax.broadcasted_iota(jnp.int32, shape, dim)


def hot(cond):
    return jnp.where(cond, 1.0, 0.0).astype(BF)


def column(row):
    return jnp.broadcast_to(row, (128, row.shape[1])).T[:, :1]


def thirds(rows):
    first = rows.astype(BF).astype(F32)
    rest = rows - first
    second = rest.astype(BF).astype(F32)
    return jnp.concatenate([first, second, rest - second, jnp.zeros_like(rows)], axis=0).astype(BF)


def joined(y):
    return y[0:8] + y[8:16] + y[16:24]


def layer(n, slides, fused, len_ref, pos_ref, tiles_hbm, wqkv_hbm, wout_hbm, cot_hbm,
          back_out, st_out, wgrad_ref, far_ref,
          tiles_ref, wqkv_ref, wout_ref, cot_ref,
          sent, psend, got, pbuf, slot_ref, st_ref, rt_ref, acc, proj, g_ref, gt_ref, kt_ref,
          vt_ref, w_ref, dp_ref, m_ref, l_ref, nt_ref, att_ref, stat_ref, kvbuf, qgbuf, stats, sbuf,
          dqt_ref, dk_ref, dv_ref, bsend, pw, wbuf, zs, zbuf,
          mask_ref, block_ref, spread_ref, back_ref, order_ref,
          in_sems, own_sems, send_sems, recv_sems, zsend, zrecv):
    me = lax.axis_index("ctx")
    my_slide = lax.axis_index("slide")
    t, d = tiles_ref.shape
    hc = wout_ref.shape[0]
    heads = hc // HD
    portion = t // n
    g = t // STRIDE
    gbits = g.bit_length() - 1
    fq = heads * g
    nf = n * g
    chunks = got.shape[0]
    wide = d // chunks

    loads = [
        pltpu.make_async_copy(src, dst, in_sems.at[i])
        for i, (src, dst) in enumerate((
            (tiles_hbm, tiles_ref), (cot_hbm, cot_ref), (wout_hbm, wout_ref), (wqkv_hbm, wqkv_ref)))
    ]
    for load in loads:
        load.start()

    barrier = pltpu.get_barrier_semaphore()

    def greet(k, carry):
        pl.semaphore_signal(barrier, inc=1, device_id={"ctx": lax.rem(me + k, n)},
                            device_id_type=MESH)
        return carry

    lax.fori_loop(1, n, greet, 0)
    if fused:
        for k in range(1, slides):
            pl.semaphore_signal(barrier, inc=1,
                                device_id={"slide": lax.rem(my_slide + k, slides)},
                                device_id_type=MESH)

    def copy_to(which, k, src, dst):
        return pltpu.make_async_remote_copy(
            src_ref=src, dst_ref=dst, send_sem=send_sems.at[which, k],
            recv_sem=recv_sems.at[which, k], device_id={"ctx": lax.rem(me + k, n)},
            device_id_type=MESH)

    def push(which, source, target):
        def body(k, carry):
            copy_to(which, k, source(lax.rem(me + k, n)), target(me)).start()
            return carry
        lax.fori_loop(1, n, body, 0)

    def landed(which, target):
        def body(k, carry):
            owner = lax.rem(me + n - k, n)
            copy_to(which, k, target(owner), target(owner)).wait_recv()
            return carry
        lax.fori_loop(1, n, body, 0)

    def left(which, target):
        def body(k, carry):
            copy_to(which, k, target(0), target(0)).wait_send()
            return carry
        lax.fori_loop(1, n, body, 0)

    length = len_ref[0]

    prow = pos_ref[...].astype(F32)
    pcol = column(prow)
    rank = jnp.sum(jnp.where(pcol < prow, 1.0, 0.0), axis=0, keepdims=True)
    down = iota((t, t), 0).astype(F32)
    across = iota((t, t), 1).astype(F32)
    pick = hot(rank == down)
    placed = column(rank) == across
    st_ref[...] = hot(placed)
    ordered = jnp.sum(jnp.where(placed, pcol, 0.0), axis=0, keepdims=True)
    psend[...] = jnp.zeros_like(psend)
    for k in range(n):
        psend[k, :, 0:portion] = jnp.broadcast_to(
            ordered[:, k * portion:(k + 1) * portion], (8, portion))
    loads[0].wait()
    for c in range(chunks):
        sent[c] = dot(pick, tiles_ref[:, c * wide:(c + 1) * wide]).astype(BF).reshape(n, portion, wide)
        if c == 0:
            pl.semaphore_wait(barrier, n - 1 + (slides - 1 if fused else 0))
            push(0, lambda peer: psend.at[peer], lambda i: pbuf.at[i])
        push(1 + c, lambda peer, c=c: sent.at[c, peer], lambda i, c=c: got.at[c, i])
    for c in range(chunks):
        got[c, me] = sent[c, me]
    pbuf[me] = psend[me]
    keep_st = pltpu.make_async_copy(st_ref, st_out, own_sems.at[0])
    keep_st.start()

    loads[1].wait()
    loads[2].wait()
    base = me * t
    live_row = base + iota((1, t), 1) < length
    live_col = base + iota((t, 1), 0) < length
    g_ref[...] = jnp.where(live_col, dot_t(cot_ref[...], wout_ref[...]), 0.0).astype(BF)
    gt_ref[...] = jnp.where(live_row, dot_t(wout_ref[...], cot_ref[...]), 0.0).astype(BF)
    gather = hot(iota((g, t), 1) >> 4 == iota((g, t), 0))
    mask_ref[...] = hot(iota((t, 1), 0) & (STRIDE - 1) == iota((1, hc), 1) >> 6)
    qgbuf[me, :, hc:2 * hc] = dot(gather, g_ref[...] * mask_ref[...]).astype(BF)
    block_ref[...] = hot(iota((fq, 1), 0) >> gbits == iota((1, hc), 1) >> 6)
    spot_col = iota((fq, 1), 0)
    spot_row = iota((1, fq), 1)
    spread_ref[...] = hot(iota((1, t), 1) == ((spot_col & (g - 1)) << 4) + (spot_col >> gbits))
    back_ref[...] = hot(iota((t, 1), 0) == ((spot_row & (g - 1)) << 4) + (spot_row >> gbits))
    m_ref[...] = jnp.zeros_like(m_ref)
    l_ref[...] = jnp.zeros_like(l_ref)
    stat_ref[...] = jnp.zeros_like(stat_ref)
    stats[...] = jnp.zeros_like(stats)
    if fused:
        run = hc // (n * slides)
        spot = iota((hc, 1), 0)
        source = (spot % (run * slides)) // run * (n * run) + spot // (run * slides) * run + spot % run
        order_ref[...] = hot(iota((1, hc), 1) == source)
        zs[...] = jnp.zeros_like(zs)
    loads[3].wait()

    landed(0, lambda i: pbuf.at[i])
    for k in range(n):
        slot_ref[:, k * portion:(k + 1) * portion] = pbuf[k, :, 0:portion]
    slot = slot_ref[0:1, :] - (me * t).astype(F32)
    rt_ref[...] = hot(column(slot) == across)
    put = hot(slot == down)
    for c in range(chunks):
        landed(1 + c, lambda i, c=c: got.at[c, i])
        sequence = dot(put, got[c].reshape(t, wide)).astype(BF)
        rows = slice(c * wide, (c + 1) * wide)
        for k in (1, 2, 0):
            cols = slice(k * hc, (k + 1) * hc)
            part = dot(sequence, wqkv_ref[rows, cols])
            if c > 0:
                part = acc[:, cols] + part
            if c < chunks - 1:
                acc[:, cols] = part
                continue
            rounded = part.astype(BF)
            proj[:, cols] = rounded
            picked = dot(gather, rounded * mask_ref[...]).astype(BF)
            if k == 0:
                qgbuf[me, :, 0:hc] = picked
                push(5, lambda peer: qgbuf.at[me], lambda i: qgbuf.at[i])
            else:
                kvbuf[me, :, (k - 1) * hc:k * hc] = picked
            if k == 2:
                push(4, lambda peer: kvbuf.at[me], lambda i: kvbuf.at[i])
    kt_ref[...] = flip(proj[:, hc:2 * hc])
    vt_ref[...] = flip(proj[:, 2 * hc:3 * hc])

    lane = iota((1, 2 * HD), 1)
    for pair in range(heads // 2):
        cols = slice(pair * 128, pair * 128 + 128)
        q2 = proj[:, cols]
        k2 = proj[:, hc + pair * 128:hc + pair * 128 + 128]
        v2 = proj[:, 2 * hc + pair * 128:2 * hc + pair * 128 + 128]
        for half in range(2):
            h = 2 * pair + half
            rows = slice(h * HD, h * HD + HD)
            mine = hot(lane >> 6 == half)
            score = jnp.where(live_col, dot_t(k2 * (mine * 0.125), q2), FLOOR)
            top = jnp.maximum(jnp.max(score, axis=0, keepdims=True), 0.5 * FLOOR)
            weight = jnp.exp(score - top)
            w_ref[h] = weight
            m_ref[h:h + 1, :] = top
            l_ref[h:h + 1, :] = jnp.sum(weight, axis=0, keepdims=True)
            nt_ref[rows, :] = dot(vt_ref[rows, :], weight.astype(BF))
            dp_ref[h] = dot(v2 * mine, gt_ref[cols, :])

    landed(4, lambda i: kvbuf.at[i])
    all_k = kvbuf[:, :, 0:hc].reshape(nf, hc)
    all_v = kvbuf[:, :, hc:2 * hc].reshape(nf, hc)
    block = block_ref[...]

    def diagonal(x):
        return jnp.concatenate([x] * heads, axis=0) * block

    own_q = diagonal(qgbuf[me, :, 0:hc])
    own_g = diagonal(qgbuf[me, :, hc:2 * hc])
    own_k = diagonal(kvbuf[me, :, 0:hc])
    own_v = diagonal(kvbuf[me, :, hc:2 * hc])
    head_rows = iota((8, fq), 0) == iota((8, fq), 1) >> gbits
    kept_cols = iota((hc, fq), 0) >> 6 == iota((hc, fq), 1) >> gbits

    def widen(row):
        return joined(dot(thirds(jnp.where(head_rows, row, 0.0)), spread_ref[...]))

    def narrow(rows):
        return jnp.sum(jnp.where(head_rows, joined(dot_t(thirds(rows), spread_ref[...])), 0.0),
                       axis=0, keepdims=True)

    def spread_cols(x):
        high, low = halves(jnp.where(kept_cols, x, 0.0))
        return dot(high, spread_ref[...]) + dot(low, spread_ref[...])

    far_live = (iota((nf, fq), 0) << 4) + (iota((nf, fq), 1) >> gbits) < length
    far_score = jnp.where(far_live, dot_t(all_k, own_q * 0.125), FLOOR)
    far_top = jnp.max(far_score, axis=0, keepdims=True)
    chosen = iota((8, t), 1) & (STRIDE - 1) == iota((8, t), 0)
    tops = m_ref[...]
    ceiling = jnp.maximum(tops, jnp.where(chosen, widen(far_top), FLOOR))
    rescale = jnp.exp(tops - ceiling)
    far_weight = jnp.where(far_live, jnp.exp(far_score - narrow(ceiling)), 0.0)
    totals = l_ref[...] * rescale + widen(jnp.sum(far_weight, axis=0, keepdims=True))
    inverse = 1.0 / jnp.where(live_row, totals, 1.0)
    inverse = jnp.where(iota((8, t), 0) < heads, inverse, 0.0)
    far_numer = spread_cols(dot(flip(all_v), far_weight.astype(BF)))
    for h in range(heads):
        rows = slice(h * HD, h * HD + HD)
        result = (nt_ref[rows, :] * rescale[h:h + 1] + far_numer[rows, :]) * inverse[h:h + 1]
        result = jnp.where(live_row, result, 0.0)
        att_ref[rows, :] = result.astype(BF)
        stat_ref[h:h + 1, :] = jnp.sum(gt_ref[rows, :].astype(F32) * result, axis=0, keepdims=True)
    stat = stat_ref[...]

    stats[0:8, :] = ceiling
    stats[8:16, :] = inverse
    stats[16:24, :] = stat
    turned = stats[...].T
    wanted = iota((t, 128), 0) & (STRIDE - 1) == iota((t, 128), 1) & 7
    sbuf[me] = jnp.sum(jnp.where(wanted, turned, 0.0).reshape(g, STRIDE, 128), axis=1)
    push(6, lambda peer: sbuf.at[me], lambda i: sbuf.at[i])

    factor = 1.0 / math.sqrt(slides * n * t)
    if fused:
        att = dot(order_ref[...], att_ref[...]).astype(BF)
        pw[...] = (dot(att, cot_ref[...]) * factor).astype(BF).reshape(n, hc // n, d)
        wbuf[me] = pw[me]
        push(7, lambda peer: pw.at[peer], lambda i: wbuf.at[i])
    else:
        wgrad_ref[...] = dot(att_ref[...], cot_ref[...]) * factor

    for pair in range(heads // 2):
        cols = slice(pair * 128, pair * 128 + 128)
        q2 = proj[:, cols] * 0.125
        g2 = g_ref[:, cols]
        key_parts = []
        value_parts = []
        for half in range(2):
            h = 2 * pair + half
            rows = slice(h * HD, h * HD + HD)
            prob = w_ref[h] * (rescale[h:h + 1] * inverse[h:h + 1])
            dscore = (prob * (dp_ref[h] - stat[h:h + 1])).astype(BF)
            dqt_ref[rows, :] = dot(kt_ref[rows, :] * 0.125, dscore)
            key_parts.append(dot(dscore, q2))
            value_parts.append(dot(prob.astype(BF), g2))
        dk_ref[:, cols] = jnp.where(lane < HD, key_parts[0], key_parts[1])
        dv_ref[:, cols] = jnp.where(lane < HD, value_parts[0], value_parts[1])

    far_prob = far_weight * narrow(inverse)
    far_dscore = far_prob * (dot_t(all_v, own_g) - narrow(stat)) * 0.125
    dqt = dqt_ref[...] + spread_cols(dot(flip(all_k), far_dscore.astype(BF)))
    proj[:, 0:hc] = dqt.T.astype(BF)
    landed(5, lambda i: qgbuf.at[i])
    all_q = qgbuf[:, :, 0:hc].reshape(nf, hc)
    all_g = qgbuf[:, :, hc:2 * hc].reshape(nf, hc)
    key_live = ((me * g + (spot_col & (g - 1))) << 4) + (spot_col >> gbits) < length
    own_score = dot_t(own_k * 0.125, all_q)
    own_dprob = dot_t(own_v, all_g)
    landed(6, lambda i: sbuf.at[i])
    rows_all = sbuf[...].reshape(nf, 128).T

    def per_head(first):
        return jnp.concatenate(
            [jnp.broadcast_to(rows_all[first + h:first + h + 1], (g, nf)) for h in range(heads)], axis=0)

    own_weight = jnp.where(key_live, jnp.exp(jnp.where(key_live, own_score - per_head(0), 0.0)), 0.0)
    own_prob = own_weight * per_head(8)
    own_dscore = own_prob * (own_dprob - per_head(16)) * 0.125
    terms = (dot(own_dscore.astype(BF), all_q), dot(own_prob.astype(BF), all_g))
    for which, base_ref in ((0, dk_ref), (1, dv_ref)):
        high, low = halves(terms[which] * block.astype(F32))
        total = base_ref[...] + dot(back_ref[...], high) + dot(back_ref[...], low)
        proj[:, (which + 1) * hc:(which + 2) * hc] = total.astype(BF)

    for c in range(chunks):
        cols = slice(c * wide, (c + 1) * wide)
        grad_seq = dot_t(proj[...], wqkv_ref[cols, :]).astype(BF)
        bsend[c] = dot(rt_ref[...], grad_seq).astype(BF).reshape(n, portion, wide)
        push(8 + c, lambda peer, c=c: bsend.at[c, peer], lambda i, cols=cols: back_out.at[i, :, cols])
    kept = [
        pltpu.make_async_copy(bsend.at[c, me], back_out.at[me, :, c * wide:(c + 1) * wide],
                              own_sems.at[1 + c]) for c in range(chunks)
    ]
    for copy in kept:
        copy.start()

    scale = math.sqrt(nf)
    for which in range(2):
        for h in range(heads):
            far_ref[which, h] = terms[which][h * g:(h + 1) * g, h * HD:(h + 1) * HD] * scale

    if fused:
        def slide_copy(k, src, dst):
            return pltpu.make_async_remote_copy(
                src_ref=src, dst_ref=dst, send_sem=zsend.at[k], recv_sem=zrecv.at[k],
                device_id={"slide": lax.rem(my_slide + k, slides)}, device_id_type=MESH)

        landed(7, lambda i: wbuf.at[i])
        summed = jnp.sum(wbuf[...].astype(F32), axis=0)
        for k in range(slides):
            zs[k, 0:run, :] = summed[k * run:(k + 1) * run, :]
        for k in range(1, slides):
            slide_copy(k, zs.at[lax.rem(my_slide + k, slides)], zbuf.at[my_slide]).start()
        zbuf[my_slide] = zs[my_slide]
        for k in range(1, slides):
            owner = lax.rem(my_slide + slides - k, slides)
            slide_copy(k, zbuf.at[owner], zbuf.at[owner]).wait_recv()
        share = jnp.sum(zbuf[...], axis=0)[0:run, :]
        for j in range(d // 128):
            wgrad_ref[pl.ds(j, run, stride=d // 128), :] = share[:, j * 128:(j + 1) * 128]
        for k in range(1, slides):
            slide_copy(k, zs.at[0], zbuf.at[0]).wait_send()
        left(7, lambda i: wbuf.at[i])
    left(0, lambda i: pbuf.at[i])
    for c in range(chunks):
        left(1 + c, lambda i, c=c: got.at[c, i])
    left(4, lambda i: kvbuf.at[i])
    left(5, lambda i: qgbuf.at[i])
    left(6, lambda i: sbuf.at[i])
    keep_st.wait()
    for copy in kept:
        copy.wait()
    for c in range(chunks):
        cols = slice(c * wide, (c + 1) * wide)
        landed(8 + c, lambda i, cols=cols: back_out.at[i, :, cols])
        left(8 + c, lambda i, c=c: bsend.at[c, i])


def local(slides, n, tiles, tile_pos, lengths, qkv_weight, out_weight, cotangent):
    _, t, d = tiles.shape
    hc = out_weight.shape[0]
    heads = hc // HD
    portion = t // n
    g = t // STRIDE
    fused = hc % (n * slides) == 0 and (hc // n) % 16 == 0
    run = hc // (n * slides) if fused else 0
    pad = -(-run // 8) * 8 if fused else 8
    wrows = hc // n if fused else 16
    chunks = 3
    wide = d // chunks
    fq = heads * g
    vm = pltpu.VMEM
    dma = pltpu.SemaphoreType.DMA
    scratch = [
        vm((t, d), BF), vm(qkv_weight.shape, BF), vm(out_weight.shape, BF), vm((t, d), BF),
        vm((chunks, n, portion, wide), BF), vm((n, 8, 128), F32), vm((chunks, n, portion, wide), BF),
        vm((n, 8, 128), F32), vm((8, t), F32), vm((t, t), BF), vm((t, t), BF),
        vm((t, 3 * hc), F32), vm((t, 3 * hc), BF), vm((t, hc), BF), vm((hc, t), BF),
        vm((hc, t), BF), vm((hc, t), BF),
        vm((heads, t, t), F32), vm((heads, t, t), F32), vm((8, t), F32), vm((8, t), F32),
        vm((hc, t), F32), vm((hc, t), BF), vm((8, t), F32),
        vm((n, g, 2 * hc), BF), vm((n, g, 2 * hc), BF), vm((128, t), F32), vm((n, g, 128), F32),
        vm((hc, t), F32), vm((t, hc), F32), vm((t, hc), F32),
        vm((chunks, n, portion, wide), BF),
        vm((n, wrows, d), BF), vm((n, wrows, d), BF),
        vm((slides, pad, d), F32), vm((slides, pad, d), F32),
        vm((t, hc), BF), vm((fq, hc), BF), vm((fq, t), BF), vm((t, fq), BF), vm((hc, hc), BF),
        dma((4,)), dma((1 + chunks,)), dma((8 + chunks, n)), dma((8 + chunks, n)),
        dma((slides,)), dma((slides,)),
    ]
    spec = pl.BlockSpec(memory_space=pltpu.VMEM)
    any_spec = pl.BlockSpec(memory_space=pl.ANY)
    back, placing, wgrad, far = pl.pallas_call(
        functools.partial(layer, n, slides, fused),
        out_shape=(
            jax.ShapeDtypeStruct((n, portion, d), BF),
            jax.ShapeDtypeStruct((t, t), BF),
            jax.ShapeDtypeStruct((run * d // 128, 128) if fused else (hc, d), F32),
            jax.ShapeDtypeStruct((2, heads, g, HD), F32),
        ),
        in_specs=[pl.BlockSpec(memory_space=pltpu.SMEM), spec] + [any_spec] * 4,
        out_specs=(any_spec, any_spec, spec, spec),
        scratch_shapes=scratch,
        compiler_params=pltpu.CompilerParams(
            collective_id=0, has_side_effects=True, vmem_limit_bytes=56 * 1024 * 1024
        ),
        cost_estimate=pl.CostEstimate(flops=8 * 10**9, bytes_accessed=6 * 10**6, transcendentals=2 * 10**6),
    )(lengths, tile_pos, tiles[0], qkv_weight, out_weight, cotangent[0])
    grads = dot(placing, back.reshape(t, d)).astype(BF)
    if fused:
        wgrad = wgrad.reshape(-1)
    else:
        wgrad = lax.psum_scatter(
            wgrad.reshape(-1), ("slide", "ctx"), scatter_dimension=0, tiled=True
        )
    return grads[None], wgrad, far[None]


def solution(mesh):
    placed = (
        P("slide", "ctx", None),
        P("slide", "ctx"),
        P("slide"),
        P(),
        P(),
        P("slide", "ctx", None),
    )
    return jax.shard_map(
        functools.partial(local, mesh.shape["slide"], mesh.shape["ctx"]),
        mesh=mesh,
        in_specs=placed,
        out_specs=(
            P("slide", "ctx", None),
            P(("slide", "ctx")),
            P("slide", None, None, "ctx", None),
        ),
        check_vma=False,
    )
```

```python
import functools
import math

import jax
import jax.numpy as jnp
from jax import lax
from jax.experimental import pallas as pl
from jax.experimental.pallas import tpu as pltpu
from jax.sharding import PartitionSpec as P

HD = 64
STRIDE = 16
FLOOR = -1e30
BF = jnp.bfloat16
F32 = jnp.float32
MESH = pl.DeviceIdType.MESH


def dot(a, b):
    return lax.dot_general(a, b, (((1,), (0,)), ((), ())), preferred_element_type=F32)


def dot_t(a, b):
    return lax.dot_general(a, b, (((1,), (1,)), ((), ())), preferred_element_type=F32)


def flip(x):
    return x.astype(F32).T.astype(BF)


def halves(x):
    high = x.astype(BF)
    return high, (x - high.astype(F32)).astype(BF)


def iota(shape, dim):
    return lax.broadcasted_iota(jnp.int32, shape, dim)


def hot(cond):
    return jnp.where(cond, 1.0, 0.0).astype(BF)


def column(row):
    return jnp.broadcast_to(row, (128, row.shape[1])).T[:, :1]


def thirds(rows):
    first = rows.astype(BF).astype(F32)
    rest = rows - first
    second = rest.astype(BF).astype(F32)
    return jnp.concatenate([first, second, rest - second, jnp.zeros_like(rows)], axis=0).astype(BF)


def joined(y):
    return y[0:8] + y[8:16] + y[16:24]


def layer(n, slides, fused, len_ref, pos_ref, tiles_hbm, wqkv_hbm, wout_hbm, cot_hbm,
          back_out, st_out, wgrad_ref, far_ref,
          tiles_ref, wqkv_ref, wout_ref, cot_ref,
          sent, psend, got, pbuf, slot_ref, st_ref, rt_ref, acc, proj, g_ref, gt_ref, kt_ref,
          vt_ref, w_ref, dp_ref, m_ref, l_ref, nt_ref, att_ref, stat_ref, kvbuf, qgbuf, stats, sbuf,
          dqt_ref, dk_ref, dv_ref, bsend, pw, wbuf, zs, zbuf,
          block_ref, spread_ref, order_ref,
          in_sems, own_sems, send_sems, recv_sems, zsend, zrecv):
    me = lax.axis_index("ctx")
    my_slide = lax.axis_index("slide")
    t, d = tiles_ref.shape
    hc = wout_ref.shape[0]
    heads = hc // HD
    portion = t // n
    g = t // STRIDE
    gbits = g.bit_length() - 1
    fq = heads * g
    nf = n * g
    chunks = got.shape[0]
    wide = d // chunks

    loads = [
        pltpu.make_async_copy(src, dst, in_sems.at[i])
        for i, (src, dst) in enumerate((
            (tiles_hbm, tiles_ref), (cot_hbm, cot_ref), (wout_hbm, wout_ref), (wqkv_hbm, wqkv_ref)))
    ]
    for load in loads:
        load.start()

    barrier = pltpu.get_barrier_semaphore()

    def greet(k, carry):
        pl.semaphore_signal(barrier, inc=1, device_id={"ctx": lax.rem(me + k, n)},
                            device_id_type=MESH)
        return carry

    lax.fori_loop(1, n, greet, 0)
    if fused:
        for k in range(1, slides):
            pl.semaphore_signal(barrier, inc=1,
                                device_id={"slide": lax.rem(my_slide + k, slides)},
                                device_id_type=MESH)

    def copy_to(which, k, src, dst):
        return pltpu.make_async_remote_copy(
            src_ref=src, dst_ref=dst, send_sem=send_sems.at[which, k],
            recv_sem=recv_sems.at[which, k], device_id={"ctx": lax.rem(me + k, n)},
            device_id_type=MESH)

    def push(which, source, target):
        def body(k, carry):
            copy_to(which, k, source(lax.rem(me + k, n)), target(me)).start()
            return carry
        lax.fori_loop(1, n, body, 0)

    def landed(which, target):
        def body(k, carry):
            owner = lax.rem(me + n - k, n)
            copy_to(which, k, target(owner), target(owner)).wait_recv()
            return carry
        lax.fori_loop(1, n, body, 0)

    def left(which, target):
        def body(k, carry):
            copy_to(which, k, target(0), target(0)).wait_send()
            return carry
        lax.fori_loop(1, n, body, 0)

    length = len_ref[0]

    prow = pos_ref[...].astype(F32)
    pcol = column(prow)
    rank = jnp.sum(jnp.where(pcol < prow, 1.0, 0.0), axis=0, keepdims=True)
    down = iota((t, t), 0).astype(F32)
    across = iota((t, t), 1).astype(F32)
    pick = hot(rank == down)
    placed = column(rank) == across
    st_ref[...] = hot(placed)
    ordered = jnp.sum(jnp.where(placed, pcol, 0.0), axis=0, keepdims=True)
    psend[...] = jnp.zeros_like(psend)
    for k in range(n):
        psend[k, :, 0:portion] = jnp.broadcast_to(
            ordered[:, k * portion:(k + 1) * portion], (8, portion))
    loads[0].wait()
    for c in range(chunks):
        sent[c] = dot(pick, tiles_ref[:, c * wide:(c + 1) * wide]).astype(BF).reshape(n, portion, wide)
        if c == 0:
            pl.semaphore_wait(barrier, n - 1 + (slides - 1 if fused else 0))
            push(0, lambda peer: psend.at[peer], lambda i: pbuf.at[i])
        push(1 + c, lambda peer, c=c: sent.at[c, peer], lambda i, c=c: got.at[c, i])
    for c in range(chunks):
        got[c, me] = sent[c, me]
    pbuf[me] = psend[me]
    keep_st = pltpu.make_async_copy(st_ref, st_out, own_sems.at[0])
    keep_st.start()

    loads[1].wait()
    loads[2].wait()
    base = me * t
    live_row = base + iota((1, t), 1) < length
    live_col = base + iota((t, 1), 0) < length
    gt_ref[...] = jnp.where(live_row, dot_t(wout_ref[...], cot_ref[...]), 0.0).astype(BF)
    lane = iota((1, 2 * HD), 1)

    pairs = heads // 2

    def fill(ref, start, value):
        for pair in range(pairs):
            ref[start + pair] = value[:, pair * 128:pair * 128 + 128]

    def taken(ref, start):
        return jnp.concatenate([ref[start + pair] for pair in range(pairs)], axis=1)

    def far_rows(start):
        parts = []
        for pair in range(pairs):
            parts.append(jnp.where(
                lane < HD,
                acc[start + pair, pl.ds(2 * pair, g, stride=STRIDE), :],
                acc[start + pair, pl.ds(2 * pair + 1, g, stride=STRIDE), :]))
        return jnp.concatenate(parts, axis=1).astype(BF)

    def add_far_rows(ref, term):
        for h in range(heads):
            cols = slice(h // 2 * 128, h // 2 * 128 + 128)
            spot = (h // 2, pl.ds(h, g, stride=STRIDE), slice(None))
            ref[spot] = ref[spot] + jnp.where(lane >> 6 == h % 2, term[h * g:(h + 1) * g, cols], 0.0)

    grad_rows = jnp.where(live_col, dot_t(cot_ref[...], wout_ref[...]), 0.0)
    fill(acc, 0, grad_rows)
    g_ref[...] = grad_rows.astype(BF)
    qgbuf[me, :, hc:2 * hc] = far_rows(0)
    block_ref[...] = hot(iota((fq, 1), 0) >> gbits == iota((1, hc), 1) >> 6)
    spot_col = iota((fq, 1), 0)
    spread_ref[...] = hot(iota((1, t), 1) == ((spot_col & (g - 1)) << 4) + (spot_col >> gbits))
    m_ref[...] = jnp.zeros_like(m_ref)
    l_ref[...] = jnp.zeros_like(l_ref)
    stat_ref[...] = jnp.zeros_like(stat_ref)
    stats[...] = jnp.zeros_like(stats)
    if fused:
        run = hc // (n * slides)
        spot = iota((hc, 1), 0)
        source = (spot % (run * slides)) // run * (n * run) + spot // (run * slides) * run + spot % run
        order_ref[...] = hot(iota((1, hc), 1) == source)
        zs[...] = jnp.zeros_like(zs)
    loads[3].wait()

    landed(0, lambda i: pbuf.at[i])
    for k in range(n):
        slot_ref[:, k * portion:(k + 1) * portion] = pbuf[k, :, 0:portion]
    slot = slot_ref[0:1, :] - (me * t).astype(F32)
    rt_ref[...] = hot(column(slot) == across)
    put = hot(slot == down)
    for c in range(chunks):
        landed(1 + c, lambda i, c=c: got.at[c, i])
        sequence = dot(put, got[c].reshape(t, wide)).astype(BF)
        rows = slice(c * wide, (c + 1) * wide)
        for k in (1, 2, 0):
            cols = slice(k * hc, (k + 1) * hc)
            part = dot(sequence, wqkv_ref[rows, cols])
            if c > 0:
                part = taken(acc, k * pairs) + part
            fill(acc, k * pairs, part)
            if c < chunks - 1:
                continue
            proj[:, cols] = part.astype(BF)
            picked = far_rows(k * pairs)
            if k == 0:
                qgbuf[me, :, 0:hc] = picked
                push(5, lambda peer: qgbuf.at[me], lambda i: qgbuf.at[i])
            else:
                kvbuf[me, :, (k - 1) * hc:k * hc] = picked
            if k == 2:
                push(4, lambda peer: kvbuf.at[me], lambda i: kvbuf.at[i])
    kt_ref[...] = flip(proj[:, hc:2 * hc])
    vt_ref[...] = flip(proj[:, 2 * hc:3 * hc])

    for pair in range(heads // 2):
        cols = slice(pair * 128, pair * 128 + 128)
        q2 = proj[:, cols]
        k2 = proj[:, hc + pair * 128:hc + pair * 128 + 128]
        v2 = proj[:, 2 * hc + pair * 128:2 * hc + pair * 128 + 128]
        for half in range(2):
            h = 2 * pair + half
            rows = slice(h * HD, h * HD + HD)
            mine = hot(lane >> 6 == half)
            score = jnp.where(live_col, dot_t(k2 * (mine * 0.125), q2), FLOOR)
            top = jnp.maximum(jnp.max(score, axis=0, keepdims=True), 0.5 * FLOOR)
            weight = jnp.exp(score - top)
            w_ref[h] = weight
            m_ref[h:h + 1, :] = top
            l_ref[h:h + 1, :] = jnp.sum(weight, axis=0, keepdims=True)
            nt_ref[rows, :] = dot(vt_ref[rows, :], weight.astype(BF))
            dp_ref[h] = dot(v2 * mine, gt_ref[cols, :])

    landed(4, lambda i: kvbuf.at[i])
    all_k = kvbuf[:, :, 0:hc].reshape(nf, hc)
    all_v = kvbuf[:, :, hc:2 * hc].reshape(nf, hc)
    block = block_ref[...]

    def diagonal(x):
        return jnp.concatenate([x] * heads, axis=0) * block

    own_q = diagonal(qgbuf[me, :, 0:hc])
    own_g = diagonal(qgbuf[me, :, hc:2 * hc])
    own_k = diagonal(kvbuf[me, :, 0:hc])
    own_v = diagonal(kvbuf[me, :, hc:2 * hc])
    head_rows = iota((8, fq), 0) == iota((8, fq), 1) >> gbits
    kept_cols = iota((hc, fq), 0) >> 6 == iota((hc, fq), 1) >> gbits

    def widen(first, second):
        rows = [thirds(jnp.where(head_rows, row, 0.0)) for row in (first, second)]
        y = dot(jnp.concatenate(rows, axis=0), spread_ref[...])
        return joined(y[0:32]), joined(y[32:64])

    def narrow(first, second):
        y = dot_t(jnp.concatenate([thirds(first), thirds(second)], axis=0), spread_ref[...])
        return [jnp.sum(jnp.where(head_rows, joined(y[k:k + 32]), 0.0), axis=0, keepdims=True)
                for k in (0, 32)]

    def spread_cols(x):
        high, low = halves(jnp.where(kept_cols, x, 0.0))
        return dot(high, spread_ref[...]) + dot(low, spread_ref[...])

    far_live = (iota((nf, fq), 0) << 4) + (iota((nf, fq), 1) >> gbits) < length
    far_score = jnp.where(far_live, dot_t(all_k, own_q * 0.125), FLOOR)
    far_top = jnp.maximum(jnp.max(far_score, axis=0, keepdims=True), 0.5 * FLOOR)
    far_weight = jnp.exp(far_score - far_top)
    far_tops, far_sums = widen(far_top, jnp.sum(far_weight, axis=0, keepdims=True))
    far_numer = spread_cols(dot(flip(all_v), far_weight.astype(BF)))
    chosen = iota((8, t), 1) & (STRIDE - 1) == iota((8, t), 0)
    tops = m_ref[...]
    far_tops = jnp.where(chosen, far_tops, FLOOR)
    ceiling = jnp.maximum(tops, far_tops)
    rescale = jnp.exp(tops - ceiling)
    far_rescale = jnp.exp(far_tops - ceiling)
    totals = l_ref[...] * rescale + far_sums * far_rescale
    inverse = 1.0 / jnp.where(live_row, totals, 1.0)
    inverse = jnp.where(iota((8, t), 0) < heads, inverse, 0.0)
    near_part = rescale * inverse
    far_part = far_rescale * inverse
    for h in range(heads):
        rows = slice(h * HD, h * HD + HD)
        result = nt_ref[rows, :] * near_part[h:h + 1] + far_numer[rows, :] * far_part[h:h + 1]
        result = jnp.where(live_row, result, 0.0)
        att_ref[rows, :] = result.astype(BF)
        stat_ref[h:h + 1, :] = jnp.sum(gt_ref[rows, :].astype(F32) * result, axis=0, keepdims=True)
    stat = stat_ref[...]

    stats[0:8, :] = ceiling
    stats[8:16, :] = inverse
    stats[16:24, :] = stat
    turned = stats[...].T
    wanted = iota((t, 128), 0) & (STRIDE - 1) == iota((t, 128), 1) & 7
    sbuf[me] = jnp.sum(jnp.where(wanted, turned, 0.0).reshape(g, STRIDE, 128), axis=1)
    push(6, lambda peer: sbuf.at[me], lambda i: sbuf.at[i])

    factor = 1.0 / math.sqrt(slides * n * t)
    if fused:
        att = dot(order_ref[...], att_ref[...]).astype(BF)
        pw[...] = (dot(att, cot_ref[...]) * factor).astype(BF).reshape(n, hc // n, d)
        wbuf[me] = pw[me]
        push(7, lambda peer: pw.at[peer], lambda i: wbuf.at[i])
    else:
        wgrad_ref[...] = dot(att_ref[...], cot_ref[...]) * factor

    for pair in range(heads // 2):
        cols = slice(pair * 128, pair * 128 + 128)
        q2 = proj[:, cols] * 0.125
        g2 = g_ref[:, cols]
        key_parts = []
        value_parts = []
        for half in range(2):
            h = 2 * pair + half
            rows = slice(h * HD, h * HD + HD)
            prob = w_ref[h] * near_part[h:h + 1]
            dscore = (prob * (dp_ref[h] - stat[h:h + 1])).astype(BF)
            dqt_ref[rows, :] = dot(kt_ref[rows, :] * 0.125, dscore)
            key_parts.append(dot(dscore, q2))
            value_parts.append(dot(prob.astype(BF), g2))
        dk_ref[pair] = jnp.where(lane < HD, key_parts[0], key_parts[1])
        dv_ref[pair] = jnp.where(lane < HD, value_parts[0], value_parts[1])

    far_unit, far_stat = narrow(far_part, stat)
    far_dscore = far_weight * far_unit * (dot_t(all_v, own_g) - far_stat)
    far_dq = dot(flip(all_k * 0.125), far_dscore.astype(BF))
    fill(acc, 0, dqt_ref[...].T)
    add_far_rows(acc, far_dq.T)
    proj[:, 0:hc] = taken(acc, 0).astype(BF)
    landed(5, lambda i: qgbuf.at[i])
    all_q = qgbuf[:, :, 0:hc].reshape(nf, hc)
    all_g = qgbuf[:, :, hc:2 * hc].reshape(nf, hc)
    key_live = ((me * g + (spot_col & (g - 1))) << 4) + (spot_col >> gbits) < length
    own_score = dot_t(own_k * 0.125, all_q)
    own_dprob = dot_t(own_v, all_g)
    landed(6, lambda i: sbuf.at[i])
    rows_all = sbuf[...].reshape(nf, 128).T

    def per_head(first):
        return jnp.concatenate(
            [jnp.broadcast_to(rows_all[first + h:first + h + 1], (g, nf)) for h in range(heads)], axis=0)

    own_weight = jnp.where(key_live, jnp.exp(jnp.where(key_live, own_score - per_head(0), 0.0)), 0.0)
    own_prob = own_weight * per_head(8)
    own_dscore = own_prob * (own_dprob - per_head(16)) * 0.125
    terms = (dot(own_dscore.astype(BF), all_q), dot(own_prob.astype(BF), all_g))
    for which, base_ref in ((0, dk_ref), (1, dv_ref)):
        add_far_rows(base_ref, terms[which])
        proj[:, (which + 1) * hc:(which + 2) * hc] = taken(base_ref, 0).astype(BF)

    for c in range(chunks):
        cols = slice(c * wide, (c + 1) * wide)
        grad_seq = dot_t(proj[...], wqkv_ref[cols, :]).astype(BF)
        bsend[c] = dot(rt_ref[...], grad_seq).astype(BF).reshape(n, portion, wide)
        push(8 + c, lambda peer, c=c: bsend.at[c, peer], lambda i, cols=cols: back_out.at[i, :, cols])
    kept = [
        pltpu.make_async_copy(bsend.at[c, me], back_out.at[me, :, c * wide:(c + 1) * wide],
                              own_sems.at[1 + c]) for c in range(chunks)
    ]
    for copy in kept:
        copy.start()

    for which in range(2):
        for h in range(heads):
            far_ref[which, h] = terms[which][h * g:(h + 1) * g, h * HD:(h + 1) * HD]

    if fused:
        def slide_copy(k, src, dst):
            return pltpu.make_async_remote_copy(
                src_ref=src, dst_ref=dst, send_sem=zsend.at[k], recv_sem=zrecv.at[k],
                device_id={"slide": lax.rem(my_slide + k, slides)}, device_id_type=MESH)

        landed(7, lambda i: wbuf.at[i])
        summed = jnp.sum(wbuf[...].astype(F32), axis=0)
        for k in range(slides):
            zs[k, 0:run, :] = summed[k * run:(k + 1) * run, :]
        for k in range(1, slides):
            slide_copy(k, zs.at[lax.rem(my_slide + k, slides)], zbuf.at[my_slide]).start()
        zbuf[my_slide] = zs[my_slide]
        for k in range(1, slides):
            owner = lax.rem(my_slide + slides - k, slides)
            slide_copy(k, zbuf.at[owner], zbuf.at[owner]).wait_recv()
        share = jnp.sum(zbuf[...], axis=0)[0:run, :]
        for j in range(d // 128):
            wgrad_ref[pl.ds(j, run, stride=d // 128), :] = share[:, j * 128:(j + 1) * 128]
        for k in range(1, slides):
            slide_copy(k, zs.at[0], zbuf.at[0]).wait_send()
        left(7, lambda i: wbuf.at[i])
    left(0, lambda i: pbuf.at[i])
    for c in range(chunks):
        left(1 + c, lambda i, c=c: got.at[c, i])
    left(4, lambda i: kvbuf.at[i])
    left(5, lambda i: qgbuf.at[i])
    left(6, lambda i: sbuf.at[i])
    keep_st.wait()
    for copy in kept:
        copy.wait()
    for c in range(chunks):
        cols = slice(c * wide, (c + 1) * wide)
        landed(8 + c, lambda i, cols=cols: back_out.at[i, :, cols])
        left(8 + c, lambda i, c=c: bsend.at[c, i])


def finish(placing_ref, back_ref, far_in, *rest):
    wgrad_in = rest[:(len(rest) - 2) // 2]
    grads_ref, far_ref = rest[len(wgrad_in):len(wgrad_in) + 2]
    grads_ref[...] = dot(placing_ref[...], back_ref[...]).astype(BF)

    @pl.when(pl.program_id(0) == 0)
    def small():
        far_ref[...] = far_in[...] * math.sqrt(far_in.shape[2] * lax.axis_size("ctx"))
        for source, target in zip(wgrad_in, rest[len(wgrad_in) + 2:]):
            target[...] = source[...]


def local(slides, n, tiles, tile_pos, lengths, qkv_weight, out_weight, cotangent):
    _, t, d = tiles.shape
    hc = out_weight.shape[0]
    heads = hc // HD
    portion = t // n
    g = t // STRIDE
    fused = hc % (n * slides) == 0 and (hc // n) % 16 == 0
    run = hc // (n * slides) if fused else 0
    pad = -(-run // 8) * 8 if fused else 8
    wrows = hc // n if fused else 16
    chunks = 3
    wide = d // chunks
    fq = heads * g
    vm = pltpu.VMEM
    dma = pltpu.SemaphoreType.DMA
    scratch = [
        vm((t, d), BF), vm(qkv_weight.shape, BF), vm(out_weight.shape, BF), vm((t, d), BF),
        vm((chunks, n, portion, wide), BF), vm((n, 8, 128), F32), vm((chunks, n, portion, wide), BF),
        vm((n, 8, 128), F32), vm((8, t), F32), vm((t, t), BF), vm((t, t), BF),
        vm((3 * hc // 128, t, 128), F32), vm((t, 3 * hc), BF), vm((t, hc), BF), vm((hc, t), BF),
        vm((hc, t), BF), vm((hc, t), BF),
        vm((heads, t, t), F32), vm((heads, t, t), F32), vm((8, t), F32), vm((8, t), F32),
        vm((hc, t), F32), vm((hc, t), BF), vm((8, t), F32),
        vm((n, g, 2 * hc), BF), vm((n, g, 2 * hc), BF), vm((128, t), F32), vm((n, g, 128), F32),
        vm((hc, t), F32), vm((heads // 2, t, 128), F32), vm((heads // 2, t, 128), F32),
        vm((chunks, n, portion, wide), BF),
        vm((n, wrows, d), BF), vm((n, wrows, d), BF),
        vm((slides, pad, d), F32), vm((slides, pad, d), F32),
        vm((fq, hc), BF), vm((fq, t), BF), vm((hc, hc), BF),
        dma((4,)), dma((1 + chunks,)), dma((8 + chunks, n)), dma((8 + chunks, n)),
        dma((slides,)), dma((slides,)),
    ]
    spec = pl.BlockSpec(memory_space=pltpu.VMEM)
    any_spec = pl.BlockSpec(memory_space=pl.ANY)
    back, placing, wgrad, far = pl.pallas_call(
        functools.partial(layer, n, slides, fused),
        out_shape=(
            jax.ShapeDtypeStruct((n, portion, d), BF),
            jax.ShapeDtypeStruct((t, t), BF),
            jax.ShapeDtypeStruct((run * d // 128, 128) if fused else (hc, d), F32),
            jax.ShapeDtypeStruct((2, heads, g, HD), F32),
        ),
        in_specs=[pl.BlockSpec(memory_space=pltpu.SMEM), spec] + [any_spec] * 4,
        out_specs=(any_spec, any_spec, spec, spec),
        scratch_shapes=scratch,
        compiler_params=pltpu.CompilerParams(
            collective_id=0, has_side_effects=True, vmem_limit_bytes=56 * 1024 * 1024
        ),
        cost_estimate=pl.CostEstimate(flops=8 * 10**9, bytes_accessed=6 * 10**6, transcendentals=2 * 10**6),
    )(lengths, tile_pos, tiles[0], qkv_weight, out_weight, cotangent[0])
    grads, far, *rest = pl.pallas_call(
        finish,
        grid=(chunks,),
        out_shape=(
            jax.ShapeDtypeStruct((t, d), BF),
            jax.ShapeDtypeStruct(far.shape, F32),
        ) + ((jax.ShapeDtypeStruct(wgrad.shape, F32),) if fused else ()),
        in_specs=[
            pl.BlockSpec((t, t), lambda i: (0, 0)),
            pl.BlockSpec((t, wide), lambda i: (0, i)),
            pl.BlockSpec(far.shape, lambda i: (0, 0, 0, 0)),
        ] + [pl.BlockSpec(wgrad.shape, lambda i: (0, 0))] * fused,
        out_specs=(
            pl.BlockSpec((t, wide), lambda i: (0, i)),
            pl.BlockSpec(far.shape, lambda i: (0, 0, 0, 0)),
        ) + (pl.BlockSpec(wgrad.shape, lambda i: (0, 0)),) * fused,
        cost_estimate=pl.CostEstimate(flops=2 * t * t * d, bytes_accessed=3 * 10**6, transcendentals=0),
    )(placing, back.reshape(t, d), far, *([wgrad] * fused))
    if fused:
        wgrad = rest[0].reshape(-1)
    else:
        wgrad = lax.psum_scatter(
            wgrad.reshape(-1), ("slide", "ctx"), scatter_dimension=0, tiled=True
        )
    return grads[None], wgrad, far[None]


def solution(mesh):
    placed = (
        P("slide", "ctx", None),
        P("slide", "ctx"),
        P("slide"),
        P(),
        P(),
        P("slide", "ctx", None),
    )
    return jax.shard_map(
        functools.partial(local, mesh.shape["slide"], mesh.shape["ctx"]),
        mesh=mesh,
        in_specs=placed,
        out_specs=(
            P("slide", "ctx", None),
            P(("slide", "ctx")),
            P("slide", None, None, "ctx", None),
        ),
        check_vma=False,
    )
```

```python
import functools
import math

import jax
import jax.numpy as jnp
from jax import lax
from jax.experimental import pallas as pl
from jax.experimental.pallas import tpu as pltpu
from jax.sharding import PartitionSpec as P

HD = 64
STRIDE = 16
FLOOR = -1e30
BF = jnp.bfloat16
F32 = jnp.float32
MESH = pl.DeviceIdType.MESH


def dot(a, b):
    return lax.dot_general(a, b, (((1,), (0,)), ((), ())), preferred_element_type=F32)


def dot_t(a, b):
    return lax.dot_general(a, b, (((1,), (1,)), ((), ())), preferred_element_type=F32)


def flip(x):
    return x.astype(F32).T.astype(BF)


def halves(x):
    high = x.astype(BF)
    return high, (x - high.astype(F32)).astype(BF)


def iota(shape, dim):
    return lax.broadcasted_iota(jnp.int32, shape, dim)


def hot(cond):
    return jnp.where(cond, 1.0, 0.0).astype(BF)


def column(row):
    return jnp.broadcast_to(row, (128, row.shape[1])).T[:, :1]


def thirds(rows):
    first = rows.astype(BF).astype(F32)
    rest = rows - first
    second = rest.astype(BF).astype(F32)
    return jnp.concatenate([first, second, rest - second, jnp.zeros_like(rows)], axis=0).astype(BF)


def joined(y):
    return y[0:8] + y[8:16] + y[16:24]


def layer(n, slides, fused, len_ref, pos_ref, tiles_hbm, wqkv_hbm, wout_hbm, cot_hbm,
          back_out, st_out, wgrad_ref, far_ref,
          tiles_ref, wqkv_ref, wout_ref, cot_ref,
          sent, psend, got, pbuf, slot_ref, st_ref, rt_ref, acc, proj, g_ref, gt_ref, kt_ref,
          vt_ref, w_ref, dp_ref, m_ref, l_ref, nt_ref, att_ref, stat_ref, kvbuf, qgbuf, stats, sbuf,
          dqt_ref, dk_ref, dv_ref, bsend, pw, wbuf, zs, zbuf, cs, cbuf,
          block_ref, spread_ref, order_ref,
          in_sems, own_sems, send_sems, recv_sems, zsend, zrecv):
    me = lax.axis_index("ctx")
    my_slide = lax.axis_index("slide")
    t, d = tiles_ref.shape
    hc = wout_ref.shape[0]
    heads = hc // HD
    portion = t // n
    g = t // STRIDE
    gbits = g.bit_length() - 1
    fq = heads * g
    nf = n * g
    chunks = got.shape[0]
    wide = d // chunks

    loads = [
        pltpu.make_async_copy(src, dst, in_sems.at[i])
        for i, (src, dst) in enumerate((
            (tiles_hbm, tiles_ref), (cot_hbm, cot_ref), (wout_hbm, wout_ref), (wqkv_hbm, wqkv_ref)))
    ]
    for load in loads:
        load.start()

    barrier = pltpu.get_barrier_semaphore()

    def greet(k, carry):
        pl.semaphore_signal(barrier, inc=1, device_id={"ctx": lax.rem(me + k, n)},
                            device_id_type=MESH)
        return carry

    lax.fori_loop(1, n, greet, 0)
    if fused:
        for k in range(1, slides):
            pl.semaphore_signal(barrier, inc=1,
                                device_id={"slide": lax.rem(my_slide + k, slides)},
                                device_id_type=MESH)

    def copy_to(which, k, src, dst):
        return pltpu.make_async_remote_copy(
            src_ref=src, dst_ref=dst, send_sem=send_sems.at[which, k],
            recv_sem=recv_sems.at[which, k], device_id={"ctx": lax.rem(me + k, n)},
            device_id_type=MESH)

    def push(which, source, target):
        def body(k, carry):
            copy_to(which, k, source(lax.rem(me + k, n)), target(me)).start()
            return carry
        lax.fori_loop(1, n, body, 0)

    def landed(which, target):
        def body(k, carry):
            owner = lax.rem(me + n - k, n)
            copy_to(which, k, target(owner), target(owner)).wait_recv()
            return carry
        lax.fori_loop(1, n, body, 0)

    def left(which, target):
        def body(k, carry):
            copy_to(which, k, target(0), target(0)).wait_send()
            return carry
        lax.fori_loop(1, n, body, 0)

    chips = n // 2
    core = lax.rem(me, 2)
    chip = lax.div(me, 2)
    partner = 2 * chip + 1 - core

    def hop(which, k, peer, src, dst):
        return pltpu.make_async_remote_copy(
            src_ref=src, dst_ref=dst, send_sem=send_sems.at[which, k],
            recv_sem=recv_sems.at[which, k], device_id={"ctx": peer}, device_id_type=MESH)

    def across_chips(k):
        return 2 * lax.rem(chip + k, chips) + core

    def behind(k, side):
        return 2 * lax.rem(chip + chips - k, chips) + side

    def spread_own(which, buf):
        def body(k, carry):
            hop(which, k, across_chips(k), buf.at[me], buf.at[me]).start()
            return carry
        lax.fori_loop(1, chips, body, 0)
        hop(which, chips, partner, buf.at[me], buf.at[me]).start()

    def hand_on(which, buf):
        def body(k, carry):
            block = buf.at[behind(k, core)]
            hop(which, k, partner, block, block).wait_recv()
            hop(which, chips + k, partner, block, block).start()
            return carry
        lax.fori_loop(1, chips, body, 0)

    def gathered(which, buf):
        hop(which, chips, partner, buf.at[partner], buf.at[partner]).wait_recv()

        def body(k, carry):
            block = buf.at[behind(k, 1 - core)]
            hop(which, chips + k, partner, block, block).wait_recv()
            return carry
        lax.fori_loop(1, chips, body, 0)

    length = len_ref[0]

    prow = pos_ref[...].astype(F32)
    pcol = column(prow)
    rank = jnp.sum(jnp.where(pcol < prow, 1.0, 0.0), axis=0, keepdims=True)
    down = iota((t, t), 0).astype(F32)
    across = iota((t, t), 1).astype(F32)
    pick = hot(rank == down)
    placed = column(rank) == across
    st_ref[...] = hot(placed)
    ordered = jnp.sum(jnp.where(placed, pcol, 0.0), axis=0, keepdims=True)
    psend[...] = jnp.zeros_like(psend)
    for k in range(n):
        psend[k, :, 0:portion] = jnp.broadcast_to(
            ordered[:, k * portion:(k + 1) * portion], (8, portion))
    loads[0].wait()
    for c in range(chunks):
        sent[c] = dot(pick, tiles_ref[:, c * wide:(c + 1) * wide]).astype(BF).reshape(n, portion, wide)
        if c == 0:
            pl.semaphore_wait(barrier, n - 1 + (slides - 1 if fused else 0))
            push(0, lambda peer: psend.at[peer], lambda i: pbuf.at[i])
        push(1 + c, lambda peer, c=c: sent.at[c, peer], lambda i, c=c: got.at[c, i])
    for c in range(chunks):
        got[c, me] = sent[c, me]
    pbuf[me] = psend[me]
    keep_st = pltpu.make_async_copy(st_ref, st_out, own_sems.at[0])
    keep_st.start()

    loads[1].wait()
    loads[2].wait()
    base = me * t
    live_row = base + iota((1, t), 1) < length
    live_col = base + iota((t, 1), 0) < length
    gt_ref[...] = jnp.where(live_row, dot_t(wout_ref[...], cot_ref[...]), 0.0).astype(BF)
    lane = iota((1, 2 * HD), 1)

    pairs = heads // 2

    def fill(ref, start, value):
        for pair in range(pairs):
            ref[start + pair] = value[:, pair * 128:pair * 128 + 128]

    def taken(ref, start):
        return jnp.concatenate([ref[start + pair] for pair in range(pairs)], axis=1)

    def far_rows(start):
        parts = []
        for pair in range(pairs):
            parts.append(jnp.where(
                lane < HD,
                acc[start + pair, pl.ds(2 * pair, g, stride=STRIDE), :],
                acc[start + pair, pl.ds(2 * pair + 1, g, stride=STRIDE), :]))
        return jnp.concatenate(parts, axis=1).astype(BF)

    def add_far_rows(ref, term):
        for h in range(heads):
            cols = slice(h // 2 * 128, h // 2 * 128 + 128)
            spot = (h // 2, pl.ds(h, g, stride=STRIDE), slice(None))
            ref[spot] = ref[spot] + jnp.where(lane >> 6 == h % 2, term[h * g:(h + 1) * g, cols], 0.0)

    grad_rows = jnp.where(live_col, dot_t(cot_ref[...], wout_ref[...]), 0.0)
    fill(acc, 0, grad_rows)
    g_ref[...] = grad_rows.astype(BF)
    qgbuf[me, :, hc:2 * hc] = far_rows(0)
    block_ref[...] = hot(iota((fq, 1), 0) >> gbits == iota((1, hc), 1) >> 6)
    spot_col = iota((fq, 1), 0)
    spread_ref[...] = hot(iota((1, t), 1) == ((spot_col & (g - 1)) << 4) + (spot_col >> gbits))
    m_ref[...] = jnp.zeros_like(m_ref)
    l_ref[...] = jnp.zeros_like(l_ref)
    stat_ref[...] = jnp.zeros_like(stat_ref)
    stats[...] = jnp.zeros_like(stats)
    if fused:
        run = hc // (n * slides)
        spot = iota((hc, 1), 0)
        side, spot = spot // (hc // 2), spot % (hc // 2)
        slab, spot = spot // (run * chips), spot % (run * chips)
        source = (slab * n + 2 * (spot // run) + side) * run + spot % run
        order_ref[...] = hot(iota((1, hc), 1) == source)
        cs[...] = jnp.zeros_like(cs)
    loads[3].wait()

    landed(0, lambda i: pbuf.at[i])
    for k in range(n):
        slot_ref[:, k * portion:(k + 1) * portion] = pbuf[k, :, 0:portion]
    slot = slot_ref[0:1, :] - (me * t).astype(F32)
    rt_ref[...] = hot(column(slot) == across)
    put = hot(slot == down)
    for c in range(chunks):
        landed(1 + c, lambda i, c=c: got.at[c, i])
        sequence = dot(put, got[c].reshape(t, wide)).astype(BF)
        rows = slice(c * wide, (c + 1) * wide)
        for k in (1, 2, 0):
            cols = slice(k * hc, (k + 1) * hc)
            part = dot(sequence, wqkv_ref[rows, cols])
            if c > 0:
                part = taken(acc, k * pairs) + part
            fill(acc, k * pairs, part)
            if c < chunks - 1:
                continue
            proj[:, cols] = part.astype(BF)
            picked = far_rows(k * pairs)
            if k == 0:
                qgbuf[me, :, 0:hc] = picked
                spread_own(5, qgbuf)
            else:
                kvbuf[me, :, (k - 1) * hc:k * hc] = picked
            if k == 2:
                spread_own(4, kvbuf)
    kt_ref[...] = flip(proj[:, hc:2 * hc])
    vt_ref[...] = flip(proj[:, 2 * hc:3 * hc])

    for pair in range(heads // 2):
        cols = slice(pair * 128, pair * 128 + 128)
        q2 = proj[:, cols]
        k2 = proj[:, hc + pair * 128:hc + pair * 128 + 128]
        v2 = proj[:, 2 * hc + pair * 128:2 * hc + pair * 128 + 128]
        for half in range(2):
            h = 2 * pair + half
            rows = slice(h * HD, h * HD + HD)
            mine = hot(lane >> 6 == half)
            score = jnp.where(live_col, dot_t(k2 * (mine * 0.125), q2), FLOOR)
            top = jnp.maximum(jnp.max(score, axis=0, keepdims=True), 0.5 * FLOOR)
            weight = jnp.exp(score - top)
            w_ref[h] = weight
            m_ref[h:h + 1, :] = top
            l_ref[h:h + 1, :] = jnp.sum(weight, axis=0, keepdims=True)
            nt_ref[rows, :] = dot(vt_ref[rows, :], weight.astype(BF))
            dp_ref[h] = dot(v2 * mine, gt_ref[cols, :])
        if pair == heads // 2 - 2:
            hand_on(4, kvbuf)

    gathered(4, kvbuf)
    all_k = kvbuf[:, :, 0:hc].reshape(nf, hc)
    all_v = kvbuf[:, :, hc:2 * hc].reshape(nf, hc)
    block = block_ref[...]

    def diagonal(x):
        return jnp.concatenate([x] * heads, axis=0) * block

    own_q = diagonal(qgbuf[me, :, 0:hc])
    own_g = diagonal(qgbuf[me, :, hc:2 * hc])
    own_k = diagonal(kvbuf[me, :, 0:hc])
    own_v = diagonal(kvbuf[me, :, hc:2 * hc])
    head_rows = iota((8, fq), 0) == iota((8, fq), 1) >> gbits
    kept_cols = iota((hc, fq), 0) >> 6 == iota((hc, fq), 1) >> gbits

    def widen(first, second):
        rows = [thirds(jnp.where(head_rows, row, 0.0)) for row in (first, second)]
        y = dot(jnp.concatenate(rows, axis=0), spread_ref[...])
        return joined(y[0:32]), joined(y[32:64])

    def narrow(first, second):
        y = dot_t(jnp.concatenate([thirds(first), thirds(second)], axis=0), spread_ref[...])
        return [jnp.sum(jnp.where(head_rows, joined(y[k:k + 32]), 0.0), axis=0, keepdims=True)
                for k in (0, 32)]

    def spread_cols(x):
        high, low = halves(jnp.where(kept_cols, x, 0.0))
        return dot(high, spread_ref[...]) + dot(low, spread_ref[...])

    far_live = (iota((nf, fq), 0) << 4) + (iota((nf, fq), 1) >> gbits) < length
    far_score = jnp.where(far_live, dot_t(all_k, own_q * 0.125), FLOOR)
    far_top = jnp.maximum(jnp.max(far_score, axis=0, keepdims=True), 0.5 * FLOOR)
    far_weight = jnp.exp(far_score - far_top)
    far_tops, far_sums = widen(far_top, jnp.sum(far_weight, axis=0, keepdims=True))
    far_numer = spread_cols(dot(flip(all_v), far_weight.astype(BF)))
    chosen = iota((8, t), 1) & (STRIDE - 1) == iota((8, t), 0)
    tops = m_ref[...]
    far_tops = jnp.where(chosen, far_tops, FLOOR)
    ceiling = jnp.maximum(tops, far_tops)
    rescale = jnp.exp(tops - ceiling)
    far_rescale = jnp.exp(far_tops - ceiling)
    totals = l_ref[...] * rescale + far_sums * far_rescale
    inverse = 1.0 / jnp.where(live_row, totals, 1.0)
    inverse = jnp.where(iota((8, t), 0) < heads, inverse, 0.0)
    near_part = rescale * inverse
    far_part = far_rescale * inverse
    for h in range(heads):
        rows = slice(h * HD, h * HD + HD)
        result = nt_ref[rows, :] * near_part[h:h + 1] + far_numer[rows, :] * far_part[h:h + 1]
        result = jnp.where(live_row, result, 0.0)
        att_ref[rows, :] = result.astype(BF)
        stat_ref[h:h + 1, :] = jnp.sum(gt_ref[rows, :].astype(F32) * result, axis=0, keepdims=True)
    stat = stat_ref[...]

    stats[0:8, :] = ceiling
    stats[8:16, :] = inverse
    stats[16:24, :] = stat
    turned = stats[...].T
    wanted = iota((t, 128), 0) & (STRIDE - 1) == iota((t, 128), 1) & 7
    sbuf[me] = jnp.sum(jnp.where(wanted, turned, 0.0).reshape(g, STRIDE, 128), axis=1)
    push(6, lambda peer: sbuf.at[me], lambda i: sbuf.at[i])

    factor = 1.0 / math.sqrt(slides * n * t)
    if fused:
        att = dot(order_ref[...], att_ref[...]).astype(BF)
        pw[...] = (dot(att, cot_ref[...]) * factor).reshape(2, hc // 2, d)
        pair_copy = hop(7, chips, partner, pw.at[1 - core], wbuf)
        pair_copy.start()
    else:
        wgrad_ref[...] = dot(att_ref[...], cot_ref[...]) * factor

    hand_on(5, qgbuf)

    def slide_copy(k, src, dst):
        return pltpu.make_async_remote_copy(
            src_ref=src, dst_ref=dst, send_sem=zsend.at[k], recv_sem=zrecv.at[k],
            device_id={"slide": lax.rem(my_slide + k, slides)}, device_id_type=MESH)

    for pair in range(heads // 2):
        cols = slice(pair * 128, pair * 128 + 128)
        q2 = proj[:, cols] * 0.125
        g2 = g_ref[:, cols]
        key_parts = []
        value_parts = []
        for half in range(2):
            h = 2 * pair + half
            rows = slice(h * HD, h * HD + HD)
            prob = w_ref[h] * near_part[h:h + 1]
            dscore = (prob * (dp_ref[h] - stat[h:h + 1])).astype(BF)
            dqt_ref[rows, :] = dot(kt_ref[rows, :] * 0.125, dscore)
            key_parts.append(dot(dscore, q2))
            value_parts.append(dot(prob.astype(BF), g2))
        dk_ref[pair] = jnp.where(lane < HD, key_parts[0], key_parts[1])
        dv_ref[pair] = jnp.where(lane < HD, value_parts[0], value_parts[1])
        if fused and pair == 0:
            pair_copy.wait_recv()
            zs[...] = (pw[core] + wbuf[...]).astype(BF).reshape(zs.shape)
            for k in range(1, slides):
                slide_copy(k, zs.at[lax.rem(my_slide + k, slides)], zbuf.at[my_slide]).start()
            zbuf[my_slide] = zs[my_slide]

    far_unit, far_stat = narrow(far_part, stat)
    far_dscore = far_weight * far_unit * (dot_t(all_v, own_g) - far_stat)
    far_dq = dot(flip(all_k * 0.125), far_dscore.astype(BF))
    fill(acc, 0, dqt_ref[...].T)
    add_far_rows(acc, far_dq.T)
    proj[:, 0:hc] = taken(acc, 0).astype(BF)
    gathered(5, qgbuf)
    all_q = qgbuf[:, :, 0:hc].reshape(nf, hc)
    all_g = qgbuf[:, :, hc:2 * hc].reshape(nf, hc)
    key_live = ((me * g + (spot_col & (g - 1))) << 4) + (spot_col >> gbits) < length
    own_score = dot_t(own_k * 0.125, all_q)
    own_dprob = dot_t(own_v, all_g)
    landed(6, lambda i: sbuf.at[i])
    rows_all = sbuf[...].reshape(nf, 128).T

    def per_head(first):
        return jnp.concatenate(
            [jnp.broadcast_to(rows_all[first + h:first + h + 1], (g, nf)) for h in range(heads)], axis=0)

    own_weight = jnp.where(key_live, jnp.exp(jnp.where(key_live, own_score - per_head(0), 0.0)), 0.0)
    own_prob = own_weight * per_head(8)
    own_dscore = own_prob * (own_dprob - per_head(16)) * 0.125
    terms = (dot(own_dscore.astype(BF), all_q), dot(own_prob.astype(BF), all_g))
    for which, base_ref in ((0, dk_ref), (1, dv_ref)):
        add_far_rows(base_ref, terms[which])
        proj[:, (which + 1) * hc:(which + 2) * hc] = taken(base_ref, 0).astype(BF)

    for c in range(chunks):
        cols = slice(c * wide, (c + 1) * wide)
        grad_seq = dot_t(proj[...], wqkv_ref[cols, :]).astype(BF)
        bsend[c] = dot(rt_ref[...], grad_seq).astype(BF).reshape(n, portion, wide)
        push(8 + c, lambda peer, c=c: bsend.at[c, peer], lambda i, cols=cols: back_out.at[i, :, cols])
    kept = [
        pltpu.make_async_copy(bsend.at[c, me], back_out.at[me, :, c * wide:(c + 1) * wide],
                              own_sems.at[1 + c]) for c in range(chunks)
    ]
    for copy in kept:
        copy.start()

    for which in range(2):
        for h in range(heads):
            far_ref[which, h] = terms[which][h * g:(h + 1) * g, h * HD:(h + 1) * HD] * math.sqrt(nf)

    if fused:
        for k in range(1, slides):
            owner = lax.rem(my_slide + slides - k, slides)
            slide_copy(k, zbuf.at[owner], zbuf.at[owner]).wait_recv()
        summed = jnp.sum(zbuf[...].astype(F32), axis=0)
        for k in range(chips):
            cs[k, 0:run, :] = summed[k * run:(k + 1) * run, :]
        for k in range(1, chips):
            hop(7, k, across_chips(k), cs.at[lax.rem(chip + k, chips)], cbuf.at[chip]).start()
        cbuf[chip] = cs[chip]
        for k in range(1, chips):
            block = cbuf.at[lax.rem(chip + chips - k, chips)]
            hop(7, k, partner, block, block).wait_recv()
        share = jnp.sum(cbuf[...], axis=0)[0:run, :]
        for j in range(d // 128):
            wgrad_ref[pl.ds(j, run, stride=d // 128), :] = share[:, j * 128:(j + 1) * 128]
        for k in range(1, slides):
            slide_copy(k, zs.at[0], zbuf.at[0]).wait_send()
        pair_copy.wait_send()
        for k in range(1, chips):
            hop(7, k, partner, cs.at[0], cs.at[0]).wait_send()
    left(0, lambda i: pbuf.at[i])
    for c in range(chunks):
        left(1 + c, lambda i, c=c: got.at[c, i])
    left(4, lambda i: kvbuf.at[i])
    left(5, lambda i: qgbuf.at[i])
    left(6, lambda i: sbuf.at[i])
    keep_st.wait()
    for copy in kept:
        copy.wait()
    for c in range(chunks):
        cols = slice(c * wide, (c + 1) * wide)
        landed(8 + c, lambda i, cols=cols: back_out.at[i, :, cols])
        left(8 + c, lambda i, c=c: bsend.at[c, i])


def finish(placing_hbm, back_hbm, *refs):
    count = (len(refs) - 6) // 2
    small_in, (grads_hbm, *small_out) = refs[:count], refs[count:2 * count + 1]
    placing_ref, back_ref, grads_ref, in_sems, out_sems, small_sems = refs[2 * count + 1:]
    chunks = back_ref.shape[0]
    wide = back_ref.shape[2]
    loads = [pltpu.make_async_copy(placing_hbm, placing_ref, in_sems.at[chunks])]
    stores = []
    for c in range(chunks):
        cols = slice(c * wide, (c + 1) * wide)
        loads.append(pltpu.make_async_copy(back_hbm.at[:, cols], back_ref.at[c], in_sems.at[c]))
        stores.append(pltpu.make_async_copy(grads_ref.at[c], grads_hbm.at[:, cols], out_sems.at[c]))
    passed = [pltpu.make_async_copy(a, b, small_sems.at[i])
              for i, (a, b) in enumerate(zip(small_in, small_out))]
    for copy in loads + passed:
        copy.start()
    loads[0].wait()
    for c in range(chunks):
        loads[1 + c].wait()
        grads_ref[c] = dot(placing_ref[...], back_ref[c]).astype(BF)
        stores[c].start()
    for copy in stores + passed:
        copy.wait()


def local(slides, n, tiles, tile_pos, lengths, qkv_weight, out_weight, cotangent):
    _, t, d = tiles.shape
    hc = out_weight.shape[0]
    heads = hc // HD
    portion = t // n
    g = t // STRIDE
    fused = hc % (n * slides) == 0 and (hc // (2 * slides)) % 16 == 0
    run = hc // (n * slides) if fused else 0
    pad = -(-run // 8) * 8 if fused else 8
    wrows = hc // 2 if fused else 16
    chunks = 3
    wide = d // chunks
    fq = heads * g
    vm = pltpu.VMEM
    dma = pltpu.SemaphoreType.DMA
    scratch = [
        vm((t, d), BF), vm(qkv_weight.shape, BF), vm(out_weight.shape, BF), vm((t, d), BF),
        vm((chunks, n, portion, wide), BF), vm((n, 8, 128), F32), vm((chunks, n, portion, wide), BF),
        vm((n, 8, 128), F32), vm((8, t), F32), vm((t, t), BF), vm((t, t), BF),
        vm((3 * hc // 128, t, 128), F32), vm((t, 3 * hc), BF), vm((t, hc), BF), vm((hc, t), BF),
        vm((hc, t), BF), vm((hc, t), BF),
        vm((heads, t, t), F32), vm((heads, t, t), F32), vm((8, t), F32), vm((8, t), F32),
        vm((hc, t), F32), vm((hc, t), BF), vm((8, t), F32),
        vm((n, g, 2 * hc), BF), vm((n, g, 2 * hc), BF), vm((128, t), F32), vm((n, g, 128), F32),
        vm((hc, t), F32), vm((heads // 2, t, 128), F32), vm((heads // 2, t, 128), F32),
        vm((chunks, n, portion, wide), BF),
        vm((2, wrows, d), F32), vm((wrows, d), F32),
        vm((slides, wrows // slides if fused else 16, d), BF),
        vm((slides, wrows // slides if fused else 16, d), BF),
        vm((n // 2, pad, d), F32), vm((n // 2, pad, d), F32),
        vm((fq, hc), BF), vm((fq, t), BF), vm((hc, hc), BF),
        dma((4,)), dma((1 + chunks,)), dma((8 + chunks, n)), dma((8 + chunks, n)),
        dma((slides,)), dma((slides,)),
    ]
    spec = pl.BlockSpec(memory_space=pltpu.VMEM)
    any_spec = pl.BlockSpec(memory_space=pl.ANY)
    back, placing, wgrad, far = pl.pallas_call(
        functools.partial(layer, n, slides, fused),
        out_shape=(
            jax.ShapeDtypeStruct((n, portion, d), BF),
            jax.ShapeDtypeStruct((t, t), BF),
            jax.ShapeDtypeStruct((run * d // 128, 128) if fused else (hc, d), F32),
            jax.ShapeDtypeStruct((2, heads, g, HD), F32),
        ),
        in_specs=[pl.BlockSpec(memory_space=pltpu.SMEM), spec] + [any_spec] * 4,
        out_specs=(any_spec, any_spec, spec, spec),
        scratch_shapes=scratch,
        compiler_params=pltpu.CompilerParams(
            collective_id=0, has_side_effects=True, vmem_limit_bytes=56 * 1024 * 1024
        ),
        cost_estimate=pl.CostEstimate(flops=8 * 10**9, bytes_accessed=6 * 10**6, transcendentals=2 * 10**6),
    )(lengths, tile_pos, tiles[0], qkv_weight, out_weight, cotangent[0])
    small = (far, wgrad) if fused else (far,)
    grads, far, *rest = pl.pallas_call(
        finish,
        out_shape=(jax.ShapeDtypeStruct((t, d), BF),)
        + tuple(jax.ShapeDtypeStruct(x.shape, F32) for x in small),
        in_specs=[any_spec] * (2 + len(small)),
        out_specs=(any_spec,) * (1 + len(small)),
        scratch_shapes=[
            vm((t, t), BF), vm((chunks, t, wide), BF), vm((chunks, t, wide), BF),
            dma((chunks + 1,)), dma((chunks,)), dma((2,)),
        ],
        compiler_params=pltpu.CompilerParams(vmem_limit_bytes=56 * 1024 * 1024),
        cost_estimate=pl.CostEstimate(flops=2 * t * t * d, bytes_accessed=3 * 10**6, transcendentals=0),
    )(placing, back.reshape(t, d), *small)
    if fused:
        wgrad = rest[0].reshape(-1)
    else:
        wgrad = lax.psum_scatter(
            wgrad.reshape(-1), ("slide", "ctx"), scatter_dimension=0, tiled=True
        )
    return grads[None], wgrad, far[None]


def solution(mesh):
    placed = (
        P("slide", "ctx", None),
        P("slide", "ctx"),
        P("slide"),
        P(),
        P(),
        P("slide", "ctx", None),
    )
    return jax.shard_map(
        functools.partial(local, mesh.shape["slide"], mesh.shape["ctx"]),
        mesh=mesh,
        in_specs=placed,
        out_specs=(
            P("slide", "ctx", None),
            P(("slide", "ctx")),
            P("slide", None, None, "ctx", None),
        ),
        check_vma=False,
    )
```

```python
import functools
import math

import jax
import jax.numpy as jnp
from jax import lax
from jax.experimental import pallas as pl
from jax.experimental.pallas import tpu as pltpu
from jax.sharding import PartitionSpec as P

HD = 64
STRIDE = 16
FLOOR = -1e30
BF = jnp.bfloat16
F32 = jnp.float32
MESH = pl.DeviceIdType.MESH


def dot(a, b):
    return lax.dot_general(a, b, (((1,), (0,)), ((), ())), preferred_element_type=F32)


def dot_t(a, b):
    return lax.dot_general(a, b, (((1,), (1,)), ((), ())), preferred_element_type=F32)


def flip(x):
    return x.astype(F32).T.astype(BF)


def halves(x):
    high = x.astype(BF)
    return high, (x - high.astype(F32)).astype(BF)


def iota(shape, dim):
    return lax.broadcasted_iota(jnp.int32, shape, dim)


def hot(cond):
    return jnp.where(cond, 1.0, 0.0).astype(BF)


def column(row):
    return jnp.broadcast_to(row, (128, row.shape[1])).T[:, :1]


def thirds(rows):
    first = rows.astype(BF).astype(F32)
    rest = rows - first
    second = rest.astype(BF).astype(F32)
    return jnp.concatenate([first, second, rest - second, jnp.zeros_like(rows)], axis=0).astype(BF)


def joined(y):
    return y[0:8] + y[8:16] + y[16:24]


def layer(n, slides, fused, len_ref, pos_ref, tiles_hbm, wqkv_hbm, wout_hbm, cot_hbm,
          back_out, st_out, wgrad_ref, far_ref,
          tiles_ref, wqkv_ref, wout_ref, cot_ref,
          sent, psend, got, pbuf, slot_ref, st_ref, rt_ref, acc, proj, g_ref, gt_ref, kt_ref,
          vt_ref, w_ref, dp_ref, m_ref, l_ref, nt_ref, att_ref, stat_ref, kvbuf, qgbuf, stats, sbuf,
          dqt_ref, dk_ref, dv_ref, bsend, pw, wbuf, zs, zbuf,
          block_ref, spread_ref, order_ref, bias_ref, wb_ref, ds_ref,
          in_sems, own_sems, send_sems, recv_sems, zsend, zrecv):
    me = lax.axis_index("ctx")
    my_slide = lax.axis_index("slide")
    t, d = tiles_ref.shape
    hc = wout_ref.shape[0]
    heads = hc // HD
    portion = t // n
    g = t // STRIDE
    gbits = g.bit_length() - 1
    fq = heads * g
    nf = n * g
    chunks = got.shape[0]
    wide = d // chunks

    loads = [
        pltpu.make_async_copy(src, dst, in_sems.at[i])
        for i, (src, dst) in enumerate((
            (tiles_hbm, tiles_ref), (cot_hbm, cot_ref), (wout_hbm, wout_ref), (wqkv_hbm, wqkv_ref)))
    ]
    for load in loads:
        load.start()

    barrier = pltpu.get_barrier_semaphore()

    def greet(k, carry):
        pl.semaphore_signal(barrier, inc=1, device_id={"ctx": lax.rem(me + k, n)},
                            device_id_type=MESH)
        return carry

    lax.fori_loop(1, n, greet, 0)
    if fused:
        for k in range(1, slides):
            pl.semaphore_signal(barrier, inc=1,
                                device_id={"slide": lax.rem(my_slide + k, slides)},
                                device_id_type=MESH)

    def copy_to(which, k, src, dst):
        return pltpu.make_async_remote_copy(
            src_ref=src, dst_ref=dst, send_sem=send_sems.at[which, k],
            recv_sem=recv_sems.at[which, k], device_id={"ctx": lax.rem(me + k, n)},
            device_id_type=MESH)

    def push(which, source, target):
        def body(k, carry):
            copy_to(which, k, source(lax.rem(me + k, n)), target(me)).start()
            return carry
        lax.fori_loop(1, n, body, 0)

    def landed(which, target):
        def body(k, carry):
            owner = lax.rem(me + n - k, n)
            copy_to(which, k, target(owner), target(owner)).wait_recv()
            return carry
        lax.fori_loop(1, n, body, 0)

    def left(which, target):
        def body(k, carry):
            copy_to(which, k, target(0), target(0)).wait_send()
            return carry
        lax.fori_loop(1, n, body, 0)

    length = len_ref[0]

    prow = pos_ref[...].astype(F32)
    pcol = column(prow)
    rank = jnp.sum(jnp.where(pcol < prow, 1.0, 0.0), axis=0, keepdims=True)
    down = iota((t, t), 0).astype(F32)
    across = iota((t, t), 1).astype(F32)
    pick = hot(rank == down)
    placed = column(rank) == across
    st_ref[...] = hot(placed)
    ordered = jnp.sum(jnp.where(placed, pcol, 0.0), axis=0, keepdims=True)
    psend[...] = jnp.zeros_like(psend)
    for k in range(n):
        psend[k, :, 0:portion] = jnp.broadcast_to(
            ordered[:, k * portion:(k + 1) * portion], (8, portion))
    loads[0].wait()
    for c in range(chunks):
        sent[c] = dot(pick, tiles_ref[:, c * wide:(c + 1) * wide]).astype(BF).reshape(n, portion, wide)
        if c == 0:
            pl.semaphore_wait(barrier, n - 1 + (slides - 1 if fused else 0))
            push(0, lambda peer: psend.at[peer], lambda i: pbuf.at[i])
        push(1 + c, lambda peer, c=c: sent.at[c, peer], lambda i, c=c: got.at[c, i])
    for c in range(chunks):
        got[c, me] = sent[c, me]
    pbuf[me] = psend[me]
    keep_st = pltpu.make_async_copy(st_ref, st_out, own_sems.at[0])
    keep_st.start()

    loads[1].wait()
    loads[2].wait()
    base = me * t
    live_row = base + iota((1, t), 1) < length
    live_col = base + iota((t, 1), 0) < length
    gt_ref[...] = jnp.where(live_row, dot_t(wout_ref[...], cot_ref[...]), 0.0).astype(BF)
    lane = iota((1, 2 * HD), 1)

    pairs = heads // 2
    bias_ref[...] = jnp.where(base + iota((t, 128), 0) < length, 0.0, FLOOR)

    def fill(ref, start, value):
        for pair in range(pairs):
            ref[start + pair] = value[:, pair * 128:pair * 128 + 128]

    def taken(ref, start):
        return jnp.concatenate([ref[start + pair] for pair in range(pairs)], axis=1)

    def far_rows(start):
        parts = []
        for pair in range(pairs):
            parts.append(jnp.where(
                lane < HD,
                acc[start + pair, pl.ds(2 * pair, g, stride=STRIDE), :],
                acc[start + pair, pl.ds(2 * pair + 1, g, stride=STRIDE), :]))
        return jnp.concatenate(parts, axis=1).astype(BF)

    def add_far_rows(ref, term):
        for h in range(heads):
            cols = slice(h // 2 * 128, h // 2 * 128 + 128)
            spot = (h // 2, pl.ds(h, g, stride=STRIDE), slice(None))
            ref[spot] = ref[spot] + jnp.where(lane >> 6 == h % 2, term[h * g:(h + 1) * g, cols], 0.0)

    grad_rows = jnp.where(live_col, dot_t(cot_ref[...], wout_ref[...]), 0.0)
    fill(acc, 0, grad_rows)
    g_ref[...] = grad_rows.astype(BF)
    qgbuf[me, :, hc:2 * hc] = far_rows(0)
    block_ref[...] = hot(iota((fq, 1), 0) >> gbits == iota((1, hc), 1) >> 6)
    spot_col = iota((fq, 1), 0)
    spread_ref[...] = hot(iota((1, t), 1) == ((spot_col & (g - 1)) << 4) + (spot_col >> gbits))
    m_ref[...] = jnp.zeros_like(m_ref)
    l_ref[...] = jnp.zeros_like(l_ref)
    stat_ref[...] = jnp.zeros_like(stat_ref)
    stats[...] = jnp.zeros_like(stats)
    if fused:
        run = hc // (n * slides)
        spot = iota((hc, 1), 0)
        source = (spot % (run * slides)) // run * (n * run) + spot // (run * slides) * run + spot % run
        order_ref[...] = hot(iota((1, hc), 1) == source)
        zs[...] = jnp.zeros_like(zs)
    loads[3].wait()

    landed(0, lambda i: pbuf.at[i])
    for k in range(n):
        slot_ref[:, k * portion:(k + 1) * portion] = pbuf[k, :, 0:portion]
    slot = slot_ref[0:1, :] - (me * t).astype(F32)
    rt_ref[...] = hot(column(slot) == across)
    put = hot(slot == down)
    for c in range(chunks):
        landed(1 + c, lambda i, c=c: got.at[c, i])
        sequence = dot(put, got[c].reshape(t, wide)).astype(BF)
        rows = slice(c * wide, (c + 1) * wide)
        for k in (1, 2, 0):
            cols = slice(k * hc, (k + 1) * hc)
            part = dot(sequence, wqkv_ref[rows, cols])
            if c > 0:
                part = taken(acc, k * pairs) + part
            fill(acc, k * pairs, part)
            if c < chunks - 1:
                continue
            proj[:, cols] = part.astype(BF)
            picked = far_rows(k * pairs)
            if k == 0:
                qgbuf[me, :, 0:hc] = picked
                push(5, lambda peer: qgbuf.at[me], lambda i: qgbuf.at[i])
            else:
                kvbuf[me, :, (k - 1) * hc:k * hc] = picked
            if k == 2:
                push(4, lambda peer: kvbuf.at[me], lambda i: kvbuf.at[i])
    kt_ref[...] = flip(proj[:, hc:2 * hc])
    vt_ref[...] = flip(proj[:, 2 * hc:3 * hc])

    span = 64
    pieces = [slice(r, r + span) for r in range(0, t, span)]

    def dead(piece):
        return jnp.concatenate([bias_ref[piece, :]] * (t // 128), axis=1)

    def folded(x, combine):
        return combine(x.reshape(span // 8, 8, t), axis=0)

    def scores(h):
        start = h // 2 * 128
        mine = hot(lane >> 6 == h % 2)
        w_ref[h] = dot_t(proj[:, hc + start:hc + start + 128] * (mine * 0.125),
                         proj[:, start:start + 128])

    scores(0)
    for h in range(heads):
        start = h // 2 * 128
        rows = slice(h * HD, h * HD + HD)
        if h + 1 < heads:
            scores(h + 1)
        dp_ref[h] = dot(proj[:, 2 * hc + start:2 * hc + start + 128] * hot(lane >> 6 == h % 2),
                        gt_ref[start:start + 128, :])
        top = jnp.full((8, t), 0.5 * FLOOR, F32)
        for piece in pieces:
            top = jnp.maximum(top, folded(w_ref[h, piece, :] + dead(piece), jnp.max))
        top = jnp.max(top, axis=0, keepdims=True)
        total = jnp.zeros((8, t), F32)
        for piece in pieces:
            weight = jnp.exp(w_ref[h, piece, :] + dead(piece) - top)
            w_ref[h, piece, :] = weight
            wb_ref[h % 2, piece, :] = weight.astype(BF)
            total = total + folded(weight, jnp.sum)
        m_ref[h:h + 1, :] = top
        l_ref[h:h + 1, :] = jnp.sum(total, axis=0, keepdims=True)
        nt_ref[rows, :] = dot(vt_ref[rows, :], wb_ref[h % 2])

    landed(4, lambda i: kvbuf.at[i])
    all_k = kvbuf[:, :, 0:hc].reshape(nf, hc)
    all_v = kvbuf[:, :, hc:2 * hc].reshape(nf, hc)
    block = block_ref[...]

    def diagonal(x):
        return jnp.concatenate([x] * heads, axis=0) * block

    own_q = diagonal(qgbuf[me, :, 0:hc])
    own_g = diagonal(qgbuf[me, :, hc:2 * hc])
    own_k = diagonal(kvbuf[me, :, 0:hc])
    own_v = diagonal(kvbuf[me, :, hc:2 * hc])
    head_rows = iota((8, fq), 0) == iota((8, fq), 1) >> gbits
    kept_cols = iota((hc, fq), 0) >> 6 == iota((hc, fq), 1) >> gbits

    def widen(first, second):
        rows = [thirds(jnp.where(head_rows, row, 0.0)) for row in (first, second)]
        y = dot(jnp.concatenate(rows, axis=0), spread_ref[...])
        return joined(y[0:32]), joined(y[32:64])

    def narrow(first, second):
        y = dot_t(jnp.concatenate([thirds(first), thirds(second)], axis=0), spread_ref[...])
        return [jnp.sum(jnp.where(head_rows, joined(y[k:k + 32]), 0.0), axis=0, keepdims=True)
                for k in (0, 32)]

    def spread_cols(x):
        high, low = halves(jnp.where(kept_cols, x, 0.0))
        return dot(high, spread_ref[...]) + dot(low, spread_ref[...])

    far_live = (iota((nf, fq), 0) << 4) + (iota((nf, fq), 1) >> gbits) < length
    far_score = jnp.where(far_live, dot_t(all_k, own_q * 0.125), FLOOR)
    far_top = jnp.maximum(jnp.max(far_score, axis=0, keepdims=True), 0.5 * FLOOR)
    far_weight = jnp.exp(far_score - far_top)
    far_tops, far_sums = widen(far_top, jnp.sum(far_weight, axis=0, keepdims=True))
    far_numer = spread_cols(dot(flip(all_v), far_weight.astype(BF)))
    chosen = iota((8, t), 1) & (STRIDE - 1) == iota((8, t), 0)
    tops = m_ref[...]
    far_tops = jnp.where(chosen, far_tops, FLOOR)
    ceiling = jnp.maximum(tops, far_tops)
    rescale = jnp.exp(tops - ceiling)
    far_rescale = jnp.exp(far_tops - ceiling)
    totals = l_ref[...] * rescale + far_sums * far_rescale
    inverse = 1.0 / jnp.where(live_row, totals, 1.0)
    inverse = jnp.where(iota((8, t), 0) < heads, inverse, 0.0)
    near_part = rescale * inverse
    far_part = far_rescale * inverse
    for h in range(heads):
        rows = slice(h * HD, h * HD + HD)
        result = nt_ref[rows, :] * near_part[h:h + 1] + far_numer[rows, :] * far_part[h:h + 1]
        result = jnp.where(live_row, result, 0.0)
        att_ref[rows, :] = result.astype(BF)
        stat_ref[h:h + 1, :] = jnp.sum(gt_ref[rows, :].astype(F32) * result, axis=0, keepdims=True)
    stat = stat_ref[...]

    stats[0:8, :] = ceiling
    stats[8:16, :] = inverse
    stats[16:24, :] = stat
    turned = stats[...].T
    wanted = iota((t, 128), 0) & (STRIDE - 1) == iota((t, 128), 1) & 7
    sbuf[me] = jnp.sum(jnp.where(wanted, turned, 0.0).reshape(g, STRIDE, 128), axis=1)
    push(6, lambda peer: sbuf.at[me], lambda i: sbuf.at[i])

    factor = 1.0 / math.sqrt(slides * n * t)
    if fused:
        att = dot(order_ref[...], att_ref[...]).astype(BF)
        pw[...] = (dot(att, cot_ref[...]) * factor).astype(BF).reshape(n, hc // n, d)
        wbuf[me] = pw[me]
        push(7, lambda peer: pw.at[peer], lambda i: wbuf.at[i])
    else:
        wgrad_ref[...] = dot(att_ref[...], cot_ref[...]) * factor

    for pair in range(heads // 2):
        cols = slice(pair * 128, pair * 128 + 128)
        q2 = proj[:, cols] * 0.125
        g2 = g_ref[:, cols]
        key_parts = []
        value_parts = []
        for half in range(2):
            h = 2 * pair + half
            rows = slice(h * HD, h * HD + HD)
            unit = near_part[h:h + 1]
            own_stat = stat[h:h + 1]
            for piece in pieces:
                prob = w_ref[h, piece, :] * unit
                wb_ref[half, piece, :] = prob.astype(BF)
                ds_ref[half, piece, :] = (prob * (dp_ref[h, piece, :] - own_stat)).astype(BF)
            dscore = ds_ref[half]
            dqt_ref[rows, :] = dot(kt_ref[rows, :] * 0.125, dscore)
            key_parts.append(dot(dscore, q2))
            value_parts.append(dot(wb_ref[half], g2))
        dk_ref[pair] = jnp.where(lane < HD, key_parts[0], key_parts[1])
        dv_ref[pair] = jnp.where(lane < HD, value_parts[0], value_parts[1])

    far_unit, far_stat = narrow(far_part, stat)
    far_dscore = far_weight * far_unit * (dot_t(all_v, own_g) - far_stat)
    far_dq = dot(flip(all_k * 0.125), far_dscore.astype(BF))
    fill(acc, 0, dqt_ref[...].T)
    add_far_rows(acc, far_dq.T)
    proj[:, 0:hc] = taken(acc, 0).astype(BF)
    landed(5, lambda i: qgbuf.at[i])
    all_q = qgbuf[:, :, 0:hc].reshape(nf, hc)
    all_g = qgbuf[:, :, hc:2 * hc].reshape(nf, hc)
    key_live = ((me * g + (spot_col & (g - 1))) << 4) + (spot_col >> gbits) < length
    own_score = dot_t(own_k * 0.125, all_q)
    own_dprob = dot_t(own_v, all_g)
    landed(6, lambda i: sbuf.at[i])
    rows_all = sbuf[...].reshape(nf, 128).T

    def per_head(first):
        return jnp.concatenate(
            [jnp.broadcast_to(rows_all[first + h:first + h + 1], (g, nf)) for h in range(heads)], axis=0)

    own_weight = jnp.where(key_live, jnp.exp(jnp.where(key_live, own_score - per_head(0), 0.0)), 0.0)
    own_prob = own_weight * per_head(8)
    own_dscore = own_prob * (own_dprob - per_head(16)) * 0.125
    terms = (dot(own_dscore.astype(BF), all_q), dot(own_prob.astype(BF), all_g))
    for which, base_ref in ((0, dk_ref), (1, dv_ref)):
        add_far_rows(base_ref, terms[which])
        proj[:, (which + 1) * hc:(which + 2) * hc] = taken(base_ref, 0).astype(BF)

    for c in range(chunks):
        cols = slice(c * wide, (c + 1) * wide)
        grad_seq = dot_t(proj[...], wqkv_ref[cols, :]).astype(BF)
        bsend[c] = dot(rt_ref[...], grad_seq).astype(BF).reshape(n, portion, wide)
        push(8 + c, lambda peer, c=c: bsend.at[c, peer], lambda i, cols=cols: back_out.at[i, :, cols])
    kept = [
        pltpu.make_async_copy(bsend.at[c, me], back_out.at[me, :, c * wide:(c + 1) * wide],
                              own_sems.at[1 + c]) for c in range(chunks)
    ]
    for copy in kept:
        copy.start()

    for which in range(2):
        for h in range(heads):
            far_ref[which, h] = terms[which][h * g:(h + 1) * g, h * HD:(h + 1) * HD] * math.sqrt(nf)

    if fused:
        def slide_copy(k, src, dst):
            return pltpu.make_async_remote_copy(
                src_ref=src, dst_ref=dst, send_sem=zsend.at[k], recv_sem=zrecv.at[k],
                device_id={"slide": lax.rem(my_slide + k, slides)}, device_id_type=MESH)

        landed(7, lambda i: wbuf.at[i])
        summed = jnp.sum(wbuf[...].astype(F32), axis=0)
        for k in range(slides):
            zs[k, 0:run, :] = summed[k * run:(k + 1) * run, :]
        for k in range(1, slides):
            slide_copy(k, zs.at[lax.rem(my_slide + k, slides)], zbuf.at[my_slide]).start()
        zbuf[my_slide] = zs[my_slide]
        for k in range(1, slides):
            owner = lax.rem(my_slide + slides - k, slides)
            slide_copy(k, zbuf.at[owner], zbuf.at[owner]).wait_recv()
        share = jnp.sum(zbuf[...], axis=0)[0:run, :]
        for j in range(d // 128):
            wgrad_ref[pl.ds(j, run, stride=d // 128), :] = share[:, j * 128:(j + 1) * 128]
        for k in range(1, slides):
            slide_copy(k, zs.at[0], zbuf.at[0]).wait_send()
        left(7, lambda i: wbuf.at[i])
    left(0, lambda i: pbuf.at[i])
    for c in range(chunks):
        left(1 + c, lambda i, c=c: got.at[c, i])
    left(4, lambda i: kvbuf.at[i])
    left(5, lambda i: qgbuf.at[i])
    left(6, lambda i: sbuf.at[i])
    keep_st.wait()
    for copy in kept:
        copy.wait()
    for c in range(chunks):
        cols = slice(c * wide, (c + 1) * wide)
        landed(8 + c, lambda i, cols=cols: back_out.at[i, :, cols])
        left(8 + c, lambda i, c=c: bsend.at[c, i])


def finish(placing_hbm, back_hbm, *refs):
    count = (len(refs) - 7) // 3
    small_in, (grads_hbm, *small_out) = refs[:count], refs[count:2 * count + 1]
    placing_ref, back_ref, grads_ref, in_sems, out_sems, small_sems = refs[2 * count + 1:2 * count + 7]
    held = refs[2 * count + 7:]
    chunks = back_ref.shape[0]
    wide = back_ref.shape[2]
    loads = [pltpu.make_async_copy(placing_hbm, placing_ref, in_sems.at[chunks])]
    stores = []
    for c in range(chunks):
        cols = slice(c * wide, (c + 1) * wide)
        loads.append(pltpu.make_async_copy(back_hbm.at[:, cols], back_ref.at[c], in_sems.at[c]))
        stores.append(pltpu.make_async_copy(grads_ref.at[c], grads_hbm.at[:, cols], out_sems.at[c]))
    taken = [pltpu.make_async_copy(a, b, small_sems.at[0, i])
             for i, (a, b) in enumerate(zip(small_in, held))]
    given = [pltpu.make_async_copy(a, b, small_sems.at[1, i])
             for i, (a, b) in enumerate(zip(held, small_out))]
    for copy in loads + taken:
        copy.start()
    loads[0].wait()
    for c in range(chunks):
        loads[1 + c].wait()
        grads_ref[c] = dot(placing_ref[...], back_ref[c]).astype(BF)
        stores[c].start()
        if c == 0:
            for before, after in zip(taken, given):
                before.wait()
                after.start()
    for copy in stores + given:
        copy.wait()


def local(slides, n, tiles, tile_pos, lengths, qkv_weight, out_weight, cotangent):
    _, t, d = tiles.shape
    hc = out_weight.shape[0]
    heads = hc // HD
    portion = t // n
    g = t // STRIDE
    fused = hc % (n * slides) == 0 and (hc // n) % 16 == 0
    run = hc // (n * slides) if fused else 0
    pad = -(-run // 8) * 8 if fused else 8
    wrows = hc // n if fused else 16
    chunks = 3
    wide = d // chunks
    fq = heads * g
    vm = pltpu.VMEM
    dma = pltpu.SemaphoreType.DMA
    scratch = [
        vm((t, d), BF), vm(qkv_weight.shape, BF), vm(out_weight.shape, BF), vm((t, d), BF),
        vm((chunks, n, portion, wide), BF), vm((n, 8, 128), F32), vm((chunks, n, portion, wide), BF),
        vm((n, 8, 128), F32), vm((8, t), F32), vm((t, t), BF), vm((t, t), BF),
        vm((3 * hc // 128, t, 128), F32), vm((t, 3 * hc), BF), vm((t, hc), BF), vm((hc, t), BF),
        vm((hc, t), BF), vm((hc, t), BF),
        vm((heads, t, t), F32), vm((heads, t, t), F32), vm((8, t), F32), vm((8, t), F32),
        vm((hc, t), F32), vm((hc, t), BF), vm((8, t), F32),
        vm((n, g, 2 * hc), BF), vm((n, g, 2 * hc), BF), vm((128, t), F32), vm((n, g, 128), F32),
        vm((hc, t), F32), vm((heads // 2, t, 128), F32), vm((heads // 2, t, 128), F32),
        vm((chunks, n, portion, wide), BF),
        vm((n, wrows, d), BF), vm((n, wrows, d), BF),
        vm((slides, pad, d), F32), vm((slides, pad, d), F32),
        vm((fq, hc), BF), vm((fq, t), BF), vm((hc, hc), BF),
        vm((t, 128), F32), vm((2, t, t), BF), vm((2, t, t), BF),
        dma((4,)), dma((1 + chunks,)), dma((8 + chunks, n)), dma((8 + chunks, n)),
        dma((slides,)), dma((slides,)),
    ]
    spec = pl.BlockSpec(memory_space=pltpu.VMEM)
    any_spec = pl.BlockSpec(memory_space=pl.ANY)
    back, placing, wgrad, far = pl.pallas_call(
        functools.partial(layer, n, slides, fused),
        out_shape=(
            jax.ShapeDtypeStruct((n, portion, d), BF),
            jax.ShapeDtypeStruct((t, t), BF),
            jax.ShapeDtypeStruct((run * d // 128, 128) if fused else (hc, d), F32),
            jax.ShapeDtypeStruct((2, heads, g, HD), F32),
        ),
        in_specs=[pl.BlockSpec(memory_space=pltpu.SMEM), spec] + [any_spec] * 4,
        out_specs=(any_spec, any_spec, spec, spec),
        scratch_shapes=scratch,
        compiler_params=pltpu.CompilerParams(
            collective_id=0, has_side_effects=True, vmem_limit_bytes=56 * 1024 * 1024
        ),
        cost_estimate=pl.CostEstimate(flops=8 * 10**9, bytes_accessed=6 * 10**6, transcendentals=2 * 10**6),
    )(lengths, tile_pos, tiles[0], qkv_weight, out_weight, cotangent[0])
    small = (far, wgrad) if fused else (far,)
    grads, far, *rest = pl.pallas_call(
        finish,
        out_shape=(jax.ShapeDtypeStruct((t, d), BF),)
        + tuple(jax.ShapeDtypeStruct(x.shape, F32) for x in small),
        in_specs=[any_spec] * (2 + len(small)),
        out_specs=(any_spec,) * (1 + len(small)),
        scratch_shapes=[
            vm((t, t), BF), vm((chunks, t, wide), BF), vm((chunks, t, wide), BF),
            dma((chunks + 1,)), dma((chunks,)), dma((2, 2)),
        ] + [vm(x.shape, F32) for x in small],
        compiler_params=pltpu.CompilerParams(vmem_limit_bytes=56 * 1024 * 1024),
        cost_estimate=pl.CostEstimate(flops=2 * t * t * d, bytes_accessed=3 * 10**6, transcendentals=0),
    )(placing, back.reshape(t, d), *small)
    if fused:
        wgrad = rest[0].reshape(-1)
    else:
        wgrad = lax.psum_scatter(
            wgrad.reshape(-1), ("slide", "ctx"), scatter_dimension=0, tiled=True
        )
    return grads[None], wgrad, far[None]


def solution(mesh):
    placed = (
        P("slide", "ctx", None),
        P("slide", "ctx"),
        P("slide"),
        P(),
        P(),
        P("slide", "ctx", None),
    )
    return jax.shard_map(
        functools.partial(local, mesh.shape["slide"], mesh.shape["ctx"]),
        mesh=mesh,
        in_specs=placed,
        out_specs=(
            P("slide", "ctx", None),
            P(("slide", "ctx")),
            P("slide", None, None, "ctx", None),
        ),
        check_vma=False,
    )
```

```python
import functools
import math

import jax
import jax.numpy as jnp
from jax import lax
from jax.experimental import pallas as pl
from jax.experimental.pallas import tpu as pltpu
from jax.sharding import PartitionSpec as P

HD = 64
STRIDE = 16
FLOOR = -1e30
BF = jnp.bfloat16
F32 = jnp.float32
MESH = pl.DeviceIdType.MESH


def dot(a, b):
    return lax.dot_general(a, b, (((1,), (0,)), ((), ())), preferred_element_type=F32)


def dot_t(a, b):
    return lax.dot_general(a, b, (((1,), (1,)), ((), ())), preferred_element_type=F32)


def flip(x):
    return x.astype(F32).T.astype(BF)


def halves(x):
    high = x.astype(BF)
    return high, (x - high.astype(F32)).astype(BF)


def iota(shape, dim):
    return lax.broadcasted_iota(jnp.int32, shape, dim)


def hot(cond):
    return jnp.where(cond, 1.0, 0.0).astype(BF)


def column(row):
    return jnp.broadcast_to(row, (128, row.shape[1])).T[:, :1]


def thirds(rows):
    first = rows.astype(BF).astype(F32)
    rest = rows - first
    second = rest.astype(BF).astype(F32)
    return jnp.concatenate([first, second, rest - second, jnp.zeros_like(rows)], axis=0).astype(BF)


def joined(y):
    return y[0:8] + y[8:16] + y[16:24]


def layer(n, slides, fused, len_ref, pos_ref, tiles_hbm, wqkv_hbm, wout_hbm, cot_hbm,
          back_out, st_out, wgrad_ref, far_ref,
          tiles_ref, wqkv_ref, wout_ref, cot_ref,
          sent, psend, got, pbuf, slot_ref, st_ref, rt_ref, acc, proj, g_ref, gt_ref, kt_ref,
          vt_ref, w_ref, dp_ref, m_ref, l_ref, nt_ref, att_ref, stat_ref, kvbuf, qgbuf, stats, sbuf,
          dqt_ref, dk_ref, dv_ref, bsend, pw, wbuf, zs, zbuf,
          block_ref, spread_ref, order_ref, bias_ref, wb_ref, ds_ref,
          in_sems, own_sems, send_sems, recv_sems, zsend, zrecv):
    me = lax.axis_index("ctx")
    my_slide = lax.axis_index("slide")
    t, d = tiles_ref.shape
    hc = wout_ref.shape[0]
    heads = hc // HD
    portion = t // n
    g = t // STRIDE
    gbits = g.bit_length() - 1
    fq = heads * g
    nf = n * g
    chunks = got.shape[0]
    wide = d // chunks

    loads = [
        pltpu.make_async_copy(src, dst, in_sems.at[i])
        for i, (src, dst) in enumerate((
            (tiles_hbm, tiles_ref), (cot_hbm, cot_ref), (wout_hbm, wout_ref), (wqkv_hbm, wqkv_ref)))
    ]
    for load in loads:
        load.start()

    barrier = pltpu.get_barrier_semaphore()

    def greet(k, carry):
        pl.semaphore_signal(barrier, inc=1, device_id={"ctx": lax.rem(me + k, n)},
                            device_id_type=MESH)
        return carry

    lax.fori_loop(1, n, greet, 0)
    if fused:
        for k in range(1, slides):
            pl.semaphore_signal(barrier, inc=1,
                                device_id={"slide": lax.rem(my_slide + k, slides)},
                                device_id_type=MESH)

    def copy_to(which, k, src, dst):
        return pltpu.make_async_remote_copy(
            src_ref=src, dst_ref=dst, send_sem=send_sems.at[which, k],
            recv_sem=recv_sems.at[which, k], device_id={"ctx": lax.rem(me + k, n)},
            device_id_type=MESH)

    def push(which, source, target):
        def body(k, carry):
            copy_to(which, k, source(lax.rem(me + k, n)), target(me)).start()
            return carry
        lax.fori_loop(1, n, body, 0)

    def landed(which, target):
        def body(k, carry):
            owner = lax.rem(me + n - k, n)
            copy_to(which, k, target(owner), target(owner)).wait_recv()
            return carry
        lax.fori_loop(1, n, body, 0)

    def left(which, target):
        def body(k, carry):
            copy_to(which, k, target(0), target(0)).wait_send()
            return carry
        lax.fori_loop(1, n, body, 0)

    length = len_ref[0]

    prow = pos_ref[...].astype(F32)
    pcol = column(prow)
    rank = jnp.sum(jnp.where(pcol < prow, 1.0, 0.0), axis=0, keepdims=True)
    down = iota((t, t), 0).astype(F32)
    across = iota((t, t), 1).astype(F32)
    pick = hot(rank == down)
    placed = column(rank) == across
    st_ref[...] = hot(placed)
    ordered = jnp.sum(jnp.where(placed, pcol, 0.0), axis=0, keepdims=True)
    psend[...] = jnp.zeros_like(psend)
    for k in range(n):
        psend[k, :, 0:portion] = jnp.broadcast_to(
            ordered[:, k * portion:(k + 1) * portion], (8, portion))
    loads[0].wait()
    for c in range(chunks):
        sent[c] = dot(pick, tiles_ref[:, c * wide:(c + 1) * wide]).astype(BF).reshape(n, portion, wide)
        if c == 0:
            pl.semaphore_wait(barrier, n - 1 + (slides - 1 if fused else 0))
            push(0, lambda peer: psend.at[peer], lambda i: pbuf.at[i])
        push(1 + c, lambda peer, c=c: sent.at[c, peer], lambda i, c=c: got.at[c, i])
    for c in range(chunks):
        got[c, me] = sent[c, me]
    pbuf[me] = psend[me]
    keep_st = pltpu.make_async_copy(st_ref, st_out, own_sems.at[0])
    keep_st.start()

    loads[1].wait()
    loads[2].wait()
    base = me * t
    live_row = base + iota((1, t), 1) < length
    live_col = base + iota((t, 1), 0) < length
    gt_ref[...] = jnp.where(live_row, dot_t(wout_ref[...], cot_ref[...]), 0.0).astype(BF)
    lane = iota((1, 2 * HD), 1)

    pairs = heads // 2
    bias_ref[...] = jnp.where(base + iota((t, 128), 0) < length, 0.0, FLOOR)

    def fill(ref, start, value):
        for pair in range(pairs):
            ref[start + pair] = value[:, pair * 128:pair * 128 + 128]

    def taken(ref, start):
        return jnp.concatenate([ref[start + pair] for pair in range(pairs)], axis=1)

    def far_rows(start):
        parts = []
        for pair in range(pairs):
            parts.append(jnp.where(
                lane < HD,
                acc[start + pair, pl.ds(2 * pair, g, stride=STRIDE), :],
                acc[start + pair, pl.ds(2 * pair + 1, g, stride=STRIDE), :]))
        return jnp.concatenate(parts, axis=1).astype(BF)

    def add_far_rows(ref, term):
        for h in range(heads):
            cols = slice(h // 2 * 128, h // 2 * 128 + 128)
            spot = (h // 2, pl.ds(h, g, stride=STRIDE), slice(None))
            ref[spot] = ref[spot] + jnp.where(lane >> 6 == h % 2, term[h * g:(h + 1) * g, cols], 0.0)

    grad_rows = jnp.where(live_col, dot_t(cot_ref[...], wout_ref[...]), 0.0)
    fill(acc, 0, grad_rows)
    g_ref[...] = grad_rows.astype(BF)
    qgbuf[me, :, hc:2 * hc] = far_rows(0)
    block_ref[...] = hot(iota((fq, 1), 0) >> gbits == iota((1, hc), 1) >> 6)
    spot_col = iota((fq, 1), 0)
    spread_ref[...] = hot(iota((1, t), 1) == ((spot_col & (g - 1)) << 4) + (spot_col >> gbits))
    m_ref[...] = jnp.zeros_like(m_ref)
    l_ref[...] = jnp.zeros_like(l_ref)
    stat_ref[...] = jnp.zeros_like(stat_ref)
    stats[...] = jnp.zeros_like(stats)
    if fused:
        run = hc // (n * slides)
        spot = iota((hc, 1), 0)
        source = (spot % (run * slides)) // run * (n * run) + spot // (run * slides) * run + spot % run
        order_ref[...] = hot(iota((1, hc), 1) == source)
        zs[...] = jnp.zeros_like(zs)
    loads[3].wait()

    landed(0, lambda i: pbuf.at[i])
    for k in range(n):
        slot_ref[:, k * portion:(k + 1) * portion] = pbuf[k, :, 0:portion]
    slot = slot_ref[0:1, :] - (me * t).astype(F32)
    rt_ref[...] = hot(column(slot) == across)
    put = hot(slot == down)
    for c in range(chunks):
        landed(1 + c, lambda i, c=c: got.at[c, i])
        sequence = dot(put, got[c].reshape(t, wide)).astype(BF)
        rows = slice(c * wide, (c + 1) * wide)
        for k in (1, 2, 0):
            cols = slice(k * hc, (k + 1) * hc)
            part = dot(sequence, wqkv_ref[rows, cols])
            if c > 0:
                part = taken(acc, k * pairs) + part
            fill(acc, k * pairs, part)
            if c < chunks - 1:
                continue
            proj[:, cols] = part.astype(BF)
            picked = far_rows(k * pairs)
            if k == 0:
                qgbuf[me, :, 0:hc] = picked
            else:
                kvbuf[me, :, (k - 1) * hc:k * hc] = picked
            if k == 2:
                push(4, lambda peer: kvbuf.at[me], lambda i: kvbuf.at[i])
    kt_ref[...] = flip(proj[:, hc:2 * hc])
    vt_ref[...] = flip(proj[:, 2 * hc:3 * hc])

    span = 64
    pieces = [slice(r, r + span) for r in range(0, t, span)]

    def dead(piece):
        return jnp.concatenate([bias_ref[piece, :]] * (t // 128), axis=1)

    def folded(x, combine):
        return combine(x.reshape(span // 8, 8, t), axis=0)

    def scores(h):
        start = h // 2 * 128
        mine = hot(lane >> 6 == h % 2)
        w_ref[h] = dot_t(proj[:, hc + start:hc + start + 128] * (mine * 0.125),
                         proj[:, start:start + 128])

    scores(0)
    for h in range(heads):
        start = h // 2 * 128
        rows = slice(h * HD, h * HD + HD)
        if h + 1 < heads:
            scores(h + 1)
        dp_ref[h] = dot(proj[:, 2 * hc + start:2 * hc + start + 128] * hot(lane >> 6 == h % 2),
                        gt_ref[start:start + 128, :])
        top = jnp.full((8, t), 0.5 * FLOOR, F32)
        for piece in pieces:
            top = jnp.maximum(top, folded(w_ref[h, piece, :] + dead(piece), jnp.max))
        top = jnp.max(top, axis=0, keepdims=True)
        total = jnp.zeros((8, t), F32)
        for piece in pieces:
            weight = jnp.exp(w_ref[h, piece, :] + dead(piece) - top)
            w_ref[h, piece, :] = weight
            wb_ref[h % 2, piece, :] = weight.astype(BF)
            total = total + folded(weight, jnp.sum)
        m_ref[h:h + 1, :] = top
        l_ref[h:h + 1, :] = jnp.sum(total, axis=0, keepdims=True)
        nt_ref[rows, :] = dot(vt_ref[rows, :], wb_ref[h % 2])

    landed(4, lambda i: kvbuf.at[i])
    push(5, lambda peer: qgbuf.at[me], lambda i: qgbuf.at[i])
    all_k = kvbuf[:, :, 0:hc].reshape(nf, hc)
    all_v = kvbuf[:, :, hc:2 * hc].reshape(nf, hc)
    block = block_ref[...]

    def diagonal(x):
        return jnp.concatenate([x] * heads, axis=0) * block

    own_q = diagonal(qgbuf[me, :, 0:hc])
    own_g = diagonal(qgbuf[me, :, hc:2 * hc])
    own_k = diagonal(kvbuf[me, :, 0:hc])
    own_v = diagonal(kvbuf[me, :, hc:2 * hc])
    head_rows = iota((8, fq), 0) == iota((8, fq), 1) >> gbits
    kept_cols = iota((hc, fq), 0) >> 6 == iota((hc, fq), 1) >> gbits

    def widen(first, second):
        rows = [thirds(jnp.where(head_rows, row, 0.0)) for row in (first, second)]
        y = dot(jnp.concatenate(rows, axis=0), spread_ref[...])
        return joined(y[0:32]), joined(y[32:64])

    def narrow(first, second):
        y = dot_t(jnp.concatenate([thirds(first), thirds(second)], axis=0), spread_ref[...])
        return [jnp.sum(jnp.where(head_rows, joined(y[k:k + 32]), 0.0), axis=0, keepdims=True)
                for k in (0, 32)]

    def spread_cols(x):
        high, low = halves(jnp.where(kept_cols, x, 0.0))
        return dot(high, spread_ref[...]) + dot(low, spread_ref[...])

    far_live = (iota((nf, fq), 0) << 4) + (iota((nf, fq), 1) >> gbits) < length
    far_score = jnp.where(far_live, dot_t(all_k, own_q * 0.125), FLOOR)
    far_top = jnp.maximum(jnp.max(far_score, axis=0, keepdims=True), 0.5 * FLOOR)
    far_weight = jnp.exp(far_score - far_top)
    far_tops, far_sums = widen(far_top, jnp.sum(far_weight, axis=0, keepdims=True))
    far_numer = spread_cols(dot(flip(all_v), far_weight.astype(BF)))
    chosen = iota((8, t), 1) & (STRIDE - 1) == iota((8, t), 0)
    tops = m_ref[...]
    far_tops = jnp.where(chosen, far_tops, FLOOR)
    ceiling = jnp.maximum(tops, far_tops)
    rescale = jnp.exp(tops - ceiling)
    far_rescale = jnp.exp(far_tops - ceiling)
    totals = l_ref[...] * rescale + far_sums * far_rescale
    inverse = 1.0 / jnp.where(live_row, totals, 1.0)
    inverse = jnp.where(iota((8, t), 0) < heads, inverse, 0.0)
    near_part = rescale * inverse
    far_part = far_rescale * inverse
    for h in range(heads):
        rows = slice(h * HD, h * HD + HD)
        result = nt_ref[rows, :] * near_part[h:h + 1] + far_numer[rows, :] * far_part[h:h + 1]
        result = jnp.where(live_row, result, 0.0)
        att_ref[rows, :] = result.astype(BF)
        stat_ref[h:h + 1, :] = jnp.sum(gt_ref[rows, :].astype(F32) * result, axis=0, keepdims=True)
    stat = stat_ref[...]

    stats[0:8, :] = ceiling
    stats[8:16, :] = inverse
    stats[16:24, :] = stat
    turned = stats[...].T
    wanted = iota((t, 128), 0) & (STRIDE - 1) == iota((t, 128), 1) & 7
    sbuf[me] = jnp.sum(jnp.where(wanted, turned, 0.0).reshape(g, STRIDE, 128), axis=1)
    push(6, lambda peer: sbuf.at[me], lambda i: sbuf.at[i])

    factor = 1.0 / math.sqrt(slides * n * t)
    if fused:
        att = dot(order_ref[...], att_ref[...]).astype(BF)
        pw[...] = (dot(att, cot_ref[...]) * factor).astype(BF).reshape(n, hc // n, d)
        wbuf[me] = pw[me]
        push(7, lambda peer: pw.at[peer], lambda i: wbuf.at[i])
    else:
        wgrad_ref[...] = dot(att_ref[...], cot_ref[...]) * factor

    for pair in range(heads // 2):
        cols = slice(pair * 128, pair * 128 + 128)
        q2 = proj[:, cols] * 0.125
        g2 = g_ref[:, cols]
        key_parts = []
        value_parts = []
        for half in range(2):
            h = 2 * pair + half
            rows = slice(h * HD, h * HD + HD)
            unit = near_part[h:h + 1]
            own_stat = stat[h:h + 1]
            for piece in pieces:
                prob = w_ref[h, piece, :] * unit
                wb_ref[half, piece, :] = prob.astype(BF)
                ds_ref[half, piece, :] = (prob * (dp_ref[h, piece, :] - own_stat)).astype(BF)
            dscore = ds_ref[half]
            dqt_ref[rows, :] = dot(kt_ref[rows, :] * 0.125, dscore)
            key_parts.append(dot(dscore, q2))
            value_parts.append(dot(wb_ref[half], g2))
        dk_ref[pair] = jnp.where(lane < HD, key_parts[0], key_parts[1])
        dv_ref[pair] = jnp.where(lane < HD, value_parts[0], value_parts[1])

    far_unit, far_stat = narrow(far_part, stat)
    far_dscore = far_weight * far_unit * (dot_t(all_v, own_g) - far_stat)
    far_dq = dot(flip(all_k * 0.125), far_dscore.astype(BF))
    fill(acc, 0, dqt_ref[...].T)
    add_far_rows(acc, far_dq.T)
    proj[:, 0:hc] = taken(acc, 0).astype(BF)
    landed(5, lambda i: qgbuf.at[i])
    all_q = qgbuf[:, :, 0:hc].reshape(nf, hc)
    all_g = qgbuf[:, :, hc:2 * hc].reshape(nf, hc)
    key_live = ((me * g + (spot_col & (g - 1))) << 4) + (spot_col >> gbits) < length
    own_score = dot_t(own_k * 0.125, all_q)
    own_dprob = dot_t(own_v, all_g)
    landed(6, lambda i: sbuf.at[i])
    rows_all = sbuf[...].reshape(nf, 128).T

    def per_head(first):
        return jnp.concatenate(
            [jnp.broadcast_to(rows_all[first + h:first + h + 1], (g, nf)) for h in range(heads)], axis=0)

    own_weight = jnp.where(key_live, jnp.exp(jnp.where(key_live, own_score - per_head(0), 0.0)), 0.0)
    own_prob = own_weight * per_head(8)
    own_dscore = own_prob * (own_dprob - per_head(16)) * 0.125
    terms = (dot(own_dscore.astype(BF), all_q), dot(own_prob.astype(BF), all_g))
    for which, base_ref in ((0, dk_ref), (1, dv_ref)):
        add_far_rows(base_ref, terms[which])
        proj[:, (which + 1) * hc:(which + 2) * hc] = taken(base_ref, 0).astype(BF)

    for c in range(chunks):
        cols = slice(c * wide, (c + 1) * wide)
        grad_seq = dot_t(proj[...], wqkv_ref[cols, :]).astype(BF)
        bsend[c] = dot(rt_ref[...], grad_seq).astype(BF).reshape(n, portion, wide)
        push(8 + c, lambda peer, c=c: bsend.at[c, peer], lambda i, cols=cols: back_out.at[i, :, cols])
    kept = [
        pltpu.make_async_copy(bsend.at[c, me], back_out.at[me, :, c * wide:(c + 1) * wide],
                              own_sems.at[1 + c]) for c in range(chunks)
    ]
    for copy in kept:
        copy.start()

    for which in range(2):
        for h in range(heads):
            far_ref[which, h] = terms[which][h * g:(h + 1) * g, h * HD:(h + 1) * HD] * math.sqrt(nf)

    if fused:
        def slide_copy(k, src, dst):
            return pltpu.make_async_remote_copy(
                src_ref=src, dst_ref=dst, send_sem=zsend.at[k], recv_sem=zrecv.at[k],
                device_id={"slide": lax.rem(my_slide + k, slides)}, device_id_type=MESH)

        landed(7, lambda i: wbuf.at[i])
        summed = jnp.sum(wbuf[...].astype(F32), axis=0)
        for k in range(slides):
            zs[k, 0:run, :] = summed[k * run:(k + 1) * run, :]
        for k in range(1, slides):
            slide_copy(k, zs.at[lax.rem(my_slide + k, slides)], zbuf.at[my_slide]).start()
        zbuf[my_slide] = zs[my_slide]
        for k in range(1, slides):
            owner = lax.rem(my_slide + slides - k, slides)
            slide_copy(k, zbuf.at[owner], zbuf.at[owner]).wait_recv()
        share = jnp.sum(zbuf[...], axis=0)[0:run, :]
        for j in range(d // 128):
            wgrad_ref[pl.ds(j, run, stride=d // 128), :] = share[:, j * 128:(j + 1) * 128]
        for k in range(1, slides):
            slide_copy(k, zs.at[0], zbuf.at[0]).wait_send()
        left(7, lambda i: wbuf.at[i])
    left(0, lambda i: pbuf.at[i])
    for c in range(chunks):
        left(1 + c, lambda i, c=c: got.at[c, i])
    left(4, lambda i: kvbuf.at[i])
    left(5, lambda i: qgbuf.at[i])
    left(6, lambda i: sbuf.at[i])
    keep_st.wait()
    for copy in kept:
        copy.wait()
    for c in range(chunks):
        cols = slice(c * wide, (c + 1) * wide)
        landed(8 + c, lambda i, cols=cols: back_out.at[i, :, cols])
        left(8 + c, lambda i, c=c: bsend.at[c, i])


def finish(placing_hbm, back_hbm, *refs):
    count = (len(refs) - 7) // 3
    small_in, (grads_hbm, *small_out) = refs[:count], refs[count:2 * count + 1]
    placing_ref, back_ref, grads_ref, in_sems, out_sems, small_sems = refs[2 * count + 1:2 * count + 7]
    held = refs[2 * count + 7:]
    chunks = back_ref.shape[0]
    wide = back_ref.shape[2]
    loads = [pltpu.make_async_copy(placing_hbm, placing_ref, in_sems.at[chunks])]
    stores = []
    for c in range(chunks):
        cols = slice(c * wide, (c + 1) * wide)
        loads.append(pltpu.make_async_copy(back_hbm.at[:, cols], back_ref.at[c], in_sems.at[c]))
        stores.append(pltpu.make_async_copy(grads_ref.at[c], grads_hbm.at[:, cols], out_sems.at[c]))
    taken = [pltpu.make_async_copy(a, b, small_sems.at[0, i])
             for i, (a, b) in enumerate(zip(small_in, held))]
    given = [pltpu.make_async_copy(a, b, small_sems.at[1, i])
             for i, (a, b) in enumerate(zip(held, small_out))]
    for copy in loads + taken:
        copy.start()
    loads[0].wait()
    for c in range(chunks):
        loads[1 + c].wait()
        grads_ref[c] = dot(placing_ref[...], back_ref[c]).astype(BF)
        stores[c].start()
        if c == 0:
            for before, after in zip(taken, given):
                before.wait()
                after.start()
    for copy in stores + given:
        copy.wait()


def local(slides, n, tiles, tile_pos, lengths, qkv_weight, out_weight, cotangent):
    _, t, d = tiles.shape
    hc = out_weight.shape[0]
    heads = hc // HD
    portion = t // n
    g = t // STRIDE
    fused = hc % (n * slides) == 0 and (hc // n) % 16 == 0
    run = hc // (n * slides) if fused else 0
    pad = -(-run // 8) * 8 if fused else 8
    wrows = hc // n if fused else 16
    chunks = 3
    wide = d // chunks
    fq = heads * g
    vm = pltpu.VMEM
    dma = pltpu.SemaphoreType.DMA
    scratch = [
        vm((t, d), BF), vm(qkv_weight.shape, BF), vm(out_weight.shape, BF), vm((t, d), BF),
        vm((chunks, n, portion, wide), BF), vm((n, 8, 128), F32), vm((chunks, n, portion, wide), BF),
        vm((n, 8, 128), F32), vm((8, t), F32), vm((t, t), BF), vm((t, t), BF),
        vm((3 * hc // 128, t, 128), F32), vm((t, 3 * hc), BF), vm((t, hc), BF), vm((hc, t), BF),
        vm((hc, t), BF), vm((hc, t), BF),
        vm((heads, t, t), F32), vm((heads, t, t), F32), vm((8, t), F32), vm((8, t), F32),
        vm((hc, t), F32), vm((hc, t), BF), vm((8, t), F32),
        vm((n, g, 2 * hc), BF), vm((n, g, 2 * hc), BF), vm((128, t), F32), vm((n, g, 128), F32),
        vm((hc, t), F32), vm((heads // 2, t, 128), F32), vm((heads // 2, t, 128), F32),
        vm((chunks, n, portion, wide), BF),
        vm((n, wrows, d), BF), vm((n, wrows, d), BF),
        vm((slides, pad, d), F32), vm((slides, pad, d), F32),
        vm((fq, hc), BF), vm((fq, t), BF), vm((hc, hc), BF),
        vm((t, 128), F32), vm((2, t, t), BF), vm((2, t, t), BF),
        dma((4,)), dma((1 + chunks,)), dma((8 + chunks, n)), dma((8 + chunks, n)),
        dma((slides,)), dma((slides,)),
    ]
    spec = pl.BlockSpec(memory_space=pltpu.VMEM)
    any_spec = pl.BlockSpec(memory_space=pl.ANY)
    back, placing, wgrad, far = pl.pallas_call(
        functools.partial(layer, n, slides, fused),
        out_shape=(
            jax.ShapeDtypeStruct((n, portion, d), BF),
            jax.ShapeDtypeStruct((t, t), BF),
            jax.ShapeDtypeStruct((run * d // 128, 128) if fused else (hc, d), F32),
            jax.ShapeDtypeStruct((2, heads, g, HD), F32),
        ),
        in_specs=[pl.BlockSpec(memory_space=pltpu.SMEM), spec] + [any_spec] * 4,
        out_specs=(any_spec, any_spec, spec, spec),
        scratch_shapes=scratch,
        compiler_params=pltpu.CompilerParams(
            collective_id=0, has_side_effects=True, vmem_limit_bytes=56 * 1024 * 1024
        ),
        cost_estimate=pl.CostEstimate(flops=8 * 10**9, bytes_accessed=6 * 10**6, transcendentals=2 * 10**6),
    )(lengths, tile_pos, tiles[0], qkv_weight, out_weight, cotangent[0])
    small = (far, wgrad) if fused else (far,)
    grads, far, *rest = pl.pallas_call(
        finish,
        out_shape=(jax.ShapeDtypeStruct((t, d), BF),)
        + tuple(jax.ShapeDtypeStruct(x.shape, F32) for x in small),
        in_specs=[any_spec] * (2 + len(small)),
        out_specs=(any_spec,) * (1 + len(small)),
        scratch_shapes=[
            vm((t, t), BF), vm((chunks, t, wide), BF), vm((chunks, t, wide), BF),
            dma((chunks + 1,)), dma((chunks,)), dma((2, 2)),
        ] + [vm(x.shape, F32) for x in small],
        compiler_params=pltpu.CompilerParams(vmem_limit_bytes=56 * 1024 * 1024),
        cost_estimate=pl.CostEstimate(flops=2 * t * t * d, bytes_accessed=3 * 10**6, transcendentals=0),
    )(placing, back.reshape(t, d), *small)
    if fused:
        wgrad = rest[0].reshape(-1)
    else:
        wgrad = lax.psum_scatter(
            wgrad.reshape(-1), ("slide", "ctx"), scatter_dimension=0, tiled=True
        )
    return grads[None], wgrad, far[None]


def solution(mesh):
    placed = (
        P("slide", "ctx", None),
        P("slide", "ctx"),
        P("slide"),
        P(),
        P(),
        P("slide", "ctx", None),
    )
    return jax.shard_map(
        functools.partial(local, mesh.shape["slide"], mesh.shape["ctx"]),
        mesh=mesh,
        in_specs=placed,
        out_specs=(
            P("slide", "ctx", None),
            P(("slide", "ctx")),
            P("slide", None, None, "ctx", None),
        ),
        check_vma=False,
    )
```
